128 devices in a mesh: dp: 4 (over x), expert: 16 (over z, y), tensor: 2 (over core).
Axes of the slice: x: 4, y: 4, z: 4, core: 2. Of those that a mesh axis runs over, the one named last changes fastest.
Arguments:
- tokens: bfloat16 [8192, 2048], P(('dp', 'expert')), may hold values from -6 to 6
- expert_ids: int32 [8192, 8], P(('dp', 'expert')), may hold values from 0 to 63, as said below
- gates: float32 [8192, 8], P(('dp', 'expert')), may hold values from 0.05 to 0.5
- token_weight: float32 [8192], P(('dp', 'expert')), may hold values from 0.25 to 4
- w_gate: bfloat16 [64, 2048, 768], P(('dp', 'expert'), None, 'tensor'), may hold values from -0.125 to 0.125
- w_up: bfloat16 [64, 2048, 768], P(('dp', 'expert'), None, 'tensor'), may hold values from -0.125 to 0.125
- w_down: bfloat16 [64, 768, 2048], P(('dp', 'expert'), 'tensor'), may hold values from -0.21875 to 0.21875
- v_gate: bfloat16 [64, 2048, 768], P(('dp', 'expert'), None, 'tensor'), may hold values from -0.125 to 0.125
- v_up: bfloat16 [64, 2048, 768], P(('dp', 'expert'), None, 'tensor'), may hold values from -0.125 to 0.125
- v_down: bfloat16 [64, 768, 2048], P(('dp', 'expert'), 'tensor'), may hold values from -0.21875 to 0.21875
Outputs:
- gv_gate: float32 [64, 2048, 768], P(('dp', 'expert'), None, 'tensor')
- gv_up: float32 [64, 2048, 768], P(('dp', 'expert'), None, 'tensor')
- gv_down: float32 [64, 768, 2048], P(('dp', 'expert'), 'tensor')
- tangent: bfloat16 [8192, 2048], P(('dp', 'expert'), 'tensor')
The draws below stay inside these ranges and needn't reach their ends.
Inputs may be any that keep to these rules, and one draw needn't show every extreme that they name: `expert_ids`: each row names 8 different experts. Among the 128 rows of one index of dp and expert (aligned blocks of rows) no expert is named more than 48 times, and one expert is named exactly 48 times by the rows of every such block.
All inputs are finite; a program needn't handle non-finite values.
Results may differ from the reference program's by a relative error of at most 0.0063.
Values may be sent and summed in bfloat16 or wider, within the bound.
No kernel may reach another device: no remote copies, remote signals or barrier semaphores. Data moves between devices by JAX's collectives and lax.ppermute only.
A program may use at most 256 MiB of HBM per device.

```python
import math
import jax
import jax.numpy as jnp
from jax import lax

D = 2048
H = 768
TOPK = 8
BLOCK = 128
TOK_DEV = 128
EXPERTS = 64
TOKENS = 8192
CAP = 48
N_TENSOR = 2


def block_choices(key, hot, share):
    others = EXPERTS - 1
    extra = CAP - share
    base = extra // others
    rest = extra % others
    key_order, key_mix, key_swing, key_tokens = jax.random.split(key, 4)
    order = jax.random.permutation(key_order, others).astype(jnp.int32)
    labels = order + (order >= hot).astype(jnp.int32)
    cuts = base + (jnp.arange(others) < rest).astype(jnp.int32)
    quota = jnp.full((EXPERTS,), share, jnp.int32)
    quota = quota.at[labels].add(-cuts)
    quota = quota.at[hot].set(CAP)
    pairs = others // 2
    mixed = jax.random.permutation(key_mix, others).astype(jnp.int32)
    mixed = mixed + (mixed >= hot).astype(jnp.int32)
    swing = jax.random.randint(key_swing, (pairs,), 0, share // 2 + 1).astype(jnp.int32)
    quota = quota.at[mixed[0:2 * pairs:2]].add(swing)
    quota = quota.at[mixed[1:2 * pairs:2]].add(-swing)
    ends = jnp.cumsum(quota)
    spots = jnp.arange(TOK_DEV * TOPK, dtype=jnp.int32)
    sequence = jnp.sum((spots[:, None] >= ends[None, :]).astype(jnp.int32), axis=1)
    chosen = sequence.reshape(TOPK, TOK_DEV).T
    shuffle = jax.random.permutation(key_tokens, TOK_DEV)
    return chosen[shuffle]


def draw_expert_ids(key, part):
    key = jax.random.fold_in(key, 11)
    blocks = TOKENS // TOK_DEV
    share = TOK_DEV * TOPK // EXPERTS
    hot = jax.random.randint(jax.random.fold_in(key, 1), (), 0, EXPERTS).astype(jnp.int32)
    keys = jax.random.split(jax.random.fold_in(key, 2), blocks)
    chosen = jax.vmap(lambda block_key: block_choices(block_key, hot, share))(keys)
    return chosen.reshape(TOKENS, TOPK).astype(jnp.int32)


def block_scale(own_key, extent, pieces, least, high):
    loudness = 1.0
    for position, shards_of in pieces:
        steps = jax.random.uniform(jax.random.fold_in(jax.random.fold_in(own_key, 6), position), (shards_of,), jnp.float32, least / len(pieces), high / len(pieces))
        loudness = loudness * jnp.repeat(jnp.exp(steps), extent[position] // shards_of).reshape((-1,) + (1,) * (len(extent) - 1 - position))
    return loudness


def bell_draw(rng, dims, deviation, limit, pieces=(), kind=jnp.bfloat16):
    factor_of = block_scale(rng, dims, pieces, -0.22, 0.18) if pieces else 1.0
    result = jax.random.normal(rng, dims, jnp.float32) * deviation * factor_of
    return jnp.minimum(jnp.maximum(result, -limit), limit).astype(kind)


def setup_inputs(seed: int = 0) -> dict:
    streams_of = jax.random.split(jax.random.key(seed), 11)
    tokens = bell_draw(streams_of[0], (TOKENS, D), 1.0, 6.0, ((0, 64),))
    expert_ids = draw_expert_ids(jax.random.fold_in(streams_of[10], 71), 0)
    gates = jnp.clip(0.05 + 0.45 * jax.random.uniform(streams_of[2], (TOKENS, TOPK), jnp.float32) ** block_scale(streams_of[2], (TOKENS, TOPK), ((0, 64),), -0.2, 0.2), 0.05, 0.5)
    token_weight = jnp.clip(jnp.exp(math.log(4.0) - 2.7725887 * jax.random.uniform(streams_of[3], (TOKENS,), jnp.float32) ** block_scale(streams_of[3], (TOKENS,), ((0, 64),), -0.2, 0.2)), 0.25, 4.0)
    w_gate = bell_draw(streams_of[4], (EXPERTS, D, H), D ** -0.5, 0.125, ((0, 64), (2, 2)))
    w_up = bell_draw(streams_of[5], (EXPERTS, D, H), D ** -0.5, 0.125, ((0, 64), (2, 2)))
    w_down = bell_draw(streams_of[6], (EXPERTS, H, D), H ** -0.5, 0.21875, ((0, 64), (1, 2)))
    v_gate = bell_draw(streams_of[7], (EXPERTS, D, H), D ** -0.5, 0.125, ((0, 64), (2, 2)))
    v_up = bell_draw(streams_of[8], (EXPERTS, D, H), D ** -0.5, 0.125, ((0, 64), (2, 2)))
    v_down = bell_draw(streams_of[9], (EXPERTS, H, D), H ** -0.5, 0.21875, ((0, 64), (1, 2)))
    return {"tokens": tokens, "expert_ids": expert_ids, "gates": gates, "token_weight": token_weight, "w_gate": w_gate, "w_up": w_up, "w_down": w_down, "v_gate": v_gate, "v_up": v_up, "v_down": v_down}


def silu_parts(pre_gate):
    sigma = jax.nn.sigmoid(pre_gate)
    return pre_gate * sigma, sigma * (1.0 + pre_gate * (1.0 - sigma))


def expert_layout(expert_ids):
    flat = expert_ids.reshape(-1).astype(jnp.int32)
    order = jnp.argsort(flat, stable=True).astype(jnp.int32)
    labels = jnp.arange(EXPERTS, dtype=jnp.int32)
    counts = jnp.sum((flat[:, None] == labels[None, :]).astype(jnp.int32), axis=0)
    starts = jnp.cumsum(counts) - counts
    return order, counts, starts


def block_rows(order, counts, starts, expert, number):
    offsets = number * BLOCK + jnp.arange(BLOCK, dtype=jnp.int32)
    valid = offsets < counts[expert]
    spots = jnp.clip(starts[expert] + offsets, 0, order.shape[0] - 1)
    flat_rows = jnp.where(valid, order[spots], 0).astype(jnp.int32)
    return flat_rows, valid


def reference(tokens, expert_ids, gates, token_weight, w_gate, w_up, w_down, v_gate, v_up, v_down):
    order, counts, starts = expert_layout(expert_ids)
    flat_gates = gates.reshape(-1)
    half = H // N_TENSOR
    zero_bf = jnp.zeros((), jnp.bfloat16)

    def gather_x(flat_rows, valid):
        owners = flat_rows // TOPK
        rows_x = jnp.where(valid[:, None], tokens[owners], zero_bf).astype(jnp.bfloat16)
        weight = jnp.where(valid, flat_gates[flat_rows], 0.0).astype(jnp.float32)
        return owners, rows_x, weight

    def forward_expert(carry, expert):
        def one_block(number, total):
            flat_rows, valid = block_rows(order, counts, starts, expert, number)
            owners, rows_x, weight = gather_x(flat_rows, valid)
            pre_gate = jnp.dot(rows_x, w_gate[expert], preferred_element_type=jnp.float32)
            pre_up = jnp.dot(rows_x, w_up[expert], preferred_element_type=jnp.float32)
            d_gate = jnp.dot(rows_x, v_gate[expert], preferred_element_type=jnp.float32)
            d_up = jnp.dot(rows_x, v_up[expert], preferred_element_type=jnp.float32)
            silu_g, slope_g = silu_parts(pre_gate)
            act = (silu_g * pre_up).astype(jnp.bfloat16)
            d_act = (slope_g * d_gate * pre_up + silu_g * d_up).astype(jnp.bfloat16)
            act_split = act.astype(jnp.float32).reshape(BLOCK, N_TENSOR, half)
            dact_split = d_act.astype(jnp.float32).reshape(BLOCK, N_TENSOR, half)
            down_split = w_down[expert].astype(jnp.float32).reshape(N_TENSOR, half, D)
            vdown_split = v_down[expert].astype(jnp.float32).reshape(N_TENSOR, half, D)
            parts = jnp.einsum("bnh,nhd->bnd", dact_split, down_split) + jnp.einsum("bnh,nhd->bnd", act_split, vdown_split)
            parts = lax.optimization_barrier(parts.astype(jnp.bfloat16)).astype(jnp.float32)
            row_sum = jnp.sum(parts, axis=1)
            return total.at[owners].add(weight[:, None] * row_sum)

        blocks = (counts[expert] + BLOCK - 1) // BLOCK
        return lax.fori_loop(0, blocks, one_block, carry), None

    dy, _ = lax.scan(forward_expert, jnp.zeros((TOKENS, D), jnp.float32), jnp.arange(EXPERTS, dtype=jnp.int32))
    tangent = dy.astype(jnp.bfloat16)
    scaled = token_weight[:, None] * dy
    factor = 1.0 / (TOK_DEV * TOPK) ** 0.5

    def backward_expert(expert):
        def one_block(number, sums):
            flat_rows, valid = block_rows(order, counts, starts, expert, number)
            owners, rows_x, weight = gather_x(flat_rows, valid)
            rows_q = (weight[:, None] * scaled[owners]).astype(jnp.bfloat16)
            pre_gate = jnp.dot(rows_x, w_gate[expert], preferred_element_type=jnp.float32)
            pre_up = jnp.dot(rows_x, w_up[expert], preferred_element_type=jnp.float32)
            silu_g, slope_g = silu_parts(pre_gate)
            act = (silu_g * pre_up).astype(jnp.bfloat16)
            back = jnp.dot(rows_q, w_down[expert].T, preferred_element_type=jnp.float32)
            grad_gate = (back * pre_up * slope_g).astype(jnp.bfloat16)
            grad_up = (back * silu_g).astype(jnp.bfloat16)
            return (sums[0] + jnp.dot(rows_x.T, grad_gate, preferred_element_type=jnp.float32),
                    sums[1] + jnp.dot(rows_x.T, grad_up, preferred_element_type=jnp.float32),
                    sums[2] + jnp.dot(act.T, rows_q, preferred_element_type=jnp.float32))

        start = (jnp.zeros((D, H), jnp.float32), jnp.zeros((D, H), jnp.float32), jnp.zeros((H, D), jnp.float32))
        blocks = (counts[expert] + BLOCK - 1) // BLOCK
        sums = lax.fori_loop(0, blocks, one_block, start)
        return (factor * sums[0], factor * sums[1], factor * sums[2])

    gv_gate, gv_up, gv_down = lax.map(backward_expert, jnp.arange(EXPERTS, dtype=jnp.int32))
    return gv_gate, gv_up, gv_down, tangent
```

```python
import jax
import jax.numpy as jnp
from jax import lax
from jax.experimental import pallas as pl
from jax.experimental.pallas import tpu as pltpu
from jax.sharding import PartitionSpec as P

BF = jnp.bfloat16
F32 = jnp.float32
GROUP = ("dp", "expert")
VMEM_LIMIT = 60 * 1024 * 1024
TILE = 256


def params():
    return pltpu.CompilerParams(
        dimension_semantics=("arbitrary",), vmem_limit_bytes=VMEM_LIMIT
    )


def cost(flops, nbytes):
    return pl.CostEstimate(flops=flops, bytes_accessed=nbytes, transcendentals=0)


def fixed(shape):
    return pl.BlockSpec(
        shape, lambda i: (0,) * len(shape), pipeline_mode=pl.Buffered(buffer_count=1)
    )


def smem():
    return pl.BlockSpec(memory_space=pltpu.SMEM)


def mm(left, right):
    return jnp.dot(left, right, preferred_element_type=F32)


def mm_t(left, right):
    return lax.dot_general(left, right, (((1,), (1,)), ((), ())), preferred_element_type=F32)


def mm_rows(left, right):
    return lax.dot_general(left, right, (((0,), (0,)), ((), ())), preferred_element_type=F32)


def spread(rows, per):
    count, toks = rows.shape
    return jnp.broadcast_to(rows[:, None, :], (count, per, toks)).reshape(count * per, toks)


def slot_match(pos, base, per):
    count, toks = pos.shape
    slot = lax.broadcasted_iota(jnp.int32, (count, per, toks), 1).reshape(count * per, toks)
    return spread(pos, per) == (slot + base).astype(F32)


def route_pack(base, ids_t, gates_t, tokens, experts, per):
    picks, toks = ids_t.shape
    width = tokens.shape[1]
    step = TILE // per
    steps = experts // step

    def kernel(base_ref, ids_ref, gates_ref, tok_ref, x_ref, pos_ref, gm_ref):
        i = pl.program_id(0)

        @pl.when(i == 0)
        def _():
            label = lax.broadcasted_iota(jnp.int32, (experts, toks), 0)
            hits = jnp.zeros((experts, toks), F32)
            gm = jnp.zeros((experts, toks), F32)
            for k in range(picks):
                match = ids_ref[k : k + 1, :] == label
                hits = jnp.where(match, 1.0, hits)
                gm = jnp.where(match, gates_ref[k : k + 1, :], gm)
            row = lax.broadcasted_iota(jnp.int32, (toks, toks), 0)
            col = lax.broadcasted_iota(jnp.int32, (toks, toks), 1)
            before = jnp.where(row < col, 1.0, 0.0).astype(BF)
            pos = mm(hits.astype(BF), before)
            pos_ref[...] = jnp.where(hits > 0.5, pos, -1.0)
            gm_ref[...] = gm

        pos = pos_ref[pl.ds(pl.multiple_of(i * step, step), step), :]
        hot = jnp.where(slot_match(pos, base_ref[0], per), 1.0, 0.0).astype(BF)
        x_ref[...] = mm(hot, tok_ref[...]).astype(BF)

    return pl.pallas_call(
        kernel,
        grid=(steps,),
        in_specs=[smem(), fixed((picks, toks)), fixed((picks, toks)), fixed((toks, width))],
        out_specs=[
            pl.BlockSpec((TILE, width), lambda i: (i, 0)),
            pl.BlockSpec((experts, toks), lambda i: (0, 0)),
            pl.BlockSpec((experts, toks), lambda i: (0, 0)),
        ],
        out_shape=[
            jax.ShapeDtypeStruct((experts * per, width), BF),
            jax.ShapeDtypeStruct((experts, toks), F32),
            jax.ShapeDtypeStruct((experts, toks), F32),
        ],
        compiler_params=params(),
        cost_estimate=cost(2 * experts * per * toks * width, 2 * experts * per * width),
        name="route_pack",
    )(base, ids_t, gates_t, tokens)


def pack(base, pos, tokens, per):
    experts, toks = pos.shape
    width = tokens.shape[1]
    step = TILE // per

    def kernel(base_ref, pos_ref, tok_ref, x_ref):
        hot = jnp.where(slot_match(pos_ref[...], base_ref[0], per), 1.0, 0.0).astype(BF)
        x_ref[...] = mm(hot, tok_ref[...]).astype(BF)

    return pl.pallas_call(
        kernel,
        grid=(experts // step,),
        in_specs=[smem(), pl.BlockSpec((step, toks), lambda i: (i, 0)), fixed((toks, width))],
        out_specs=pl.BlockSpec((TILE, width), lambda i: (i, 0)),
        out_shape=jax.ShapeDtypeStruct((experts * per, width), BF),
        compiler_params=params(),
        cost_estimate=cost(2 * experts * per * toks * width, 2 * experts * per * width),
        name="pack",
    )(base, pos, tokens)


def forward(rows, mats, hidden):
    count, width = rows.shape

    def kernel(x_ref, w_ref, ad_ref, silu_ref, us_ref):
        pre = mm(x_ref[...], w_ref[...])
        gate = pre[:, :hidden]
        up = pre[:, hidden : 2 * hidden]
        d_gate = pre[:, 2 * hidden : 3 * hidden]
        d_up = pre[:, 3 * hidden :]
        sigma = jax.nn.sigmoid(gate)
        silu = gate * sigma
        us = sigma * (1.0 + gate * (1.0 - sigma)) * up
        ad_ref[:, :hidden] = (silu * up).astype(BF)
        ad_ref[:, hidden:] = (us * d_gate + silu * d_up).astype(BF)
        silu_ref[...] = silu
        us_ref[...] = us

    return pl.pallas_call(
        kernel,
        grid=(count // TILE,),
        in_specs=[pl.BlockSpec((TILE, width), lambda i: (i, 0)), fixed((width, 4 * hidden))],
        out_specs=[
            pl.BlockSpec((TILE, 2 * hidden), lambda i: (i, 0)),
            pl.BlockSpec((TILE, hidden), lambda i: (i, 0)),
            pl.BlockSpec((TILE, hidden), lambda i: (i, 0)),
        ],
        out_shape=[
            jax.ShapeDtypeStruct((count, 2 * hidden), BF),
            jax.ShapeDtypeStruct((count, hidden), F32),
            jax.ShapeDtypeStruct((count, hidden), F32),
        ],
        compiler_params=params(),
        cost_estimate=cost(8 * count * width * hidden, 2 * count * width + 12 * count * hidden),
        name="forward",
    )(rows, mats)


def part_rows(ad_own, ad_other, down_own, down_other):
    count, inner = ad_own.shape
    width = down_own.shape[1]

    def kernel(a_ref, b_ref, wa_ref, wb_ref, out_ref):
        out_ref[...] = (mm(a_ref[...], wa_ref[...]) + mm(b_ref[...], wb_ref[...])).astype(BF)

    return pl.pallas_call(
        kernel,
        grid=(count // TILE,),
        in_specs=[
            pl.BlockSpec((TILE, inner), lambda i: (i, 0)),
            pl.BlockSpec((TILE, inner), lambda i: (i, 0)),
            fixed((inner, width)),
            fixed((inner, width)),
        ],
        out_specs=pl.BlockSpec((TILE, width), lambda i: (i, 0)),
        out_shape=jax.ShapeDtypeStruct((count, width), BF),
        compiler_params=params(),
        cost_estimate=cost(4 * count * width * inner, 2 * count * width + 4 * inner * width),
        name="part_rows",
    )(ad_own, ad_other, down_own, down_other)


def split_gates(pos, gm, base, per):
    weight = jnp.where(slot_match(pos, base, per), spread(gm, per), 0.0)
    high = weight.astype(BF)
    low = (weight - high.astype(F32)).astype(BF)
    return high, low


def combine(base, pos, gm, rows, start, per):
    experts, toks = pos.shape
    width = rows.shape[1]
    step = TILE // per
    steps = experts // step
    first = start is None

    def kernel(base_ref, pos_ref, gm_ref, rows_ref, *rest):
        start_ref = None if first else rest[0]
        out_ref, acc_ref = rest[-2:]
        i = pl.program_id(0)
        high, low = split_gates(pos_ref[...], gm_ref[...], base_ref[0], per)
        term = mm_rows(jnp.concatenate([high, low], axis=1), rows_ref[...])

        @pl.when(i == 0)
        def _():
            acc_ref[...] = term

        @pl.when(i > 0)
        def _():
            acc_ref[...] += term

        @pl.when(i == steps - 1)
        def _():
            total = acc_ref[:toks, :] + acc_ref[toks:, :]
            out_ref[...] = total if first else total + start_ref[...]

    extra = [] if first else [start]
    return pl.pallas_call(
        kernel,
        grid=(steps,),
        in_specs=[
            smem(),
            pl.BlockSpec((step, toks), lambda i: (i, 0)),
            pl.BlockSpec((step, toks), lambda i: (i, 0)),
            pl.BlockSpec((TILE, width), lambda i: (i, 0)),
        ]
        + [fixed((toks, width)) for _ in extra],
        out_specs=pl.BlockSpec((toks, width), lambda i: (0, 0)),
        out_shape=jax.ShapeDtypeStruct((toks, width), F32),
        scratch_shapes=[pltpu.VMEM((2 * toks, width), F32)],
        compiler_params=params(),
        cost_estimate=cost(4 * experts * per * toks * width, 2 * experts * per * width),
        name="combine",
    )(base, pos, gm, rows, *extra)


def weigh_pack(base, pos, gm, weight, own, other, per, half):
    experts, toks = pos.shape
    width = own.shape[1]
    step = TILE // per

    def kernel(base_ref, pos_ref, gm_ref, tw_ref, own_ref, other_ref, q_ref, *rest):
        high_ref, low_ref = rest[-2:]

        @pl.when(pl.program_id(0) == 0)
        def _():
            if half:
                cols = pl.ds(pl.multiple_of(base_ref[1] * half, half), half)
                rest[0][...] = (own_ref[:, cols] + other_ref[:, cols]).astype(BF)
            scaled = tw_ref[...] * (own_ref[...] + other_ref[...])
            high = scaled.astype(BF)
            high_ref[...] = high
            low_ref[...] = (scaled - high.astype(F32)).astype(BF)

        g_high, g_low = split_gates(pos_ref[...], gm_ref[...], base_ref[0], per)
        q_ref[...] = (
            mm(g_high, high_ref[...]) + mm(g_low, high_ref[...]) + mm(g_high, low_ref[...])
        ).astype(BF)

    out_specs = [pl.BlockSpec((TILE, width), lambda i: (i, 0))]
    out_shape = [jax.ShapeDtypeStruct((experts * per, width), BF)]
    if half:
        out_specs.append(pl.BlockSpec((toks, half), lambda i: (0, 0)))
        out_shape.append(jax.ShapeDtypeStruct((toks, half), BF))
    return pl.pallas_call(
        kernel,
        grid=(experts // step,),
        in_specs=[
            smem(),
            pl.BlockSpec((step, toks), lambda i: (i, 0)),
            pl.BlockSpec((step, toks), lambda i: (i, 0)),
            fixed((toks, 1)),
            fixed((toks, width)),
            fixed((toks, width)),
        ],
        out_specs=out_specs,
        out_shape=out_shape,
        scratch_shapes=[pltpu.VMEM((toks, width), BF), pltpu.VMEM((toks, width), BF)],
        compiler_params=params(),
        cost_estimate=cost(6 * experts * per * toks * width, 2 * experts * per * width),
        name="weigh_pack",
    )(base, pos, gm, weight, own, other)


def backward(own, other, down, sums, factor):
    count, width = own[0].shape
    hidden = down.shape[0]
    steps = count // TILE
    last = factor is not None
    piece = 256

    def kernel(*refs):
        own_refs, other_refs = refs[:5], refs[5:10]
        down_ref = refs[10]
        i = pl.program_id(0)
        if last:
            in_g, in_d = refs[11:13]
            gate_out, up_out, down_out, acc_g = refs[13:]
            acc_d = down_out.at[0]
        else:
            acc_g, acc_d = refs[11:]

        def terms(tile):
            q_ref, x_ref, ad_ref, silu_ref, us_ref = tile
            q = q_ref[...]
            back = mm_t(q, down_ref[...])
            grads = jnp.concatenate(
                [(back * us_ref[...]).astype(BF), (back * silu_ref[...]).astype(BF)], axis=1
            )
            return mm_rows(grads, x_ref[...]), mm_rows(ad_ref[:, :hidden], q)

        @pl.when(i == 0)
        def _():
            term_g, term_d = terms(own_refs)
            acc_g[...] = term_g + in_g[...] if last else term_g
            acc_d[...] = term_d + in_d[...] if last else term_d

        @pl.when((i > 0) & (i < steps))
        def _():
            term_g, term_d = terms(own_refs)
            acc_g[...] += term_g
            acc_d[...] += term_d

        @pl.when(i >= steps)
        def _():
            term_g, term_d = terms(other_refs)
            acc_g[...] += term_g
            acc_d[...] += term_d

        if last:

            @pl.when(i == 2 * steps - 1)
            def _():
                for start in range(0, width, piece):
                    cols = slice(start, start + piece)
                    gate_out[0, cols, :] = factor * acc_g[:hidden, cols].T
                    up_out[0, cols, :] = factor * acc_g[hidden:, cols].T
                acc_d[...] = factor * acc_d[...]

    def tiles(arrays, index):
        return [pl.BlockSpec((TILE, a.shape[1]), lambda i: (index(i), 0)) for a in arrays]

    in_specs = (
        tiles(own, lambda i: jnp.minimum(i, steps - 1))
        + tiles(other, lambda i: jnp.maximum(i - steps, 0))
        + [fixed((hidden, width))]
    )
    scratch = []
    if last:
        in_specs += [fixed((2 * hidden, width)), fixed((hidden, width))]
        shapes = [(1, width, hidden), (1, width, hidden), (1, hidden, width)]
        scratch = [pltpu.VMEM((2 * hidden, width), F32)]
    else:
        shapes = [(2 * hidden, width), (hidden, width)]
    return pl.pallas_call(
        kernel,
        grid=(2 * steps,),
        in_specs=in_specs,
        out_specs=[fixed(shape) for shape in shapes],
        out_shape=[jax.ShapeDtypeStruct(shape, F32) for shape in shapes],
        scratch_shapes=scratch,
        compiler_params=params(),
        cost_estimate=cost(16 * count * width * hidden, 8 * count * width),
        name="backward",
    )(*own, *other, down, *sums)


def exchange(rows):
    return lax.all_to_all(rows, GROUP, split_axis=0, concat_axis=0, tiled=True)


def body(tokens, expert_ids, gates, token_weight, w_gate, w_up, w_down, v_gate, v_up, v_down):
    toks, width = tokens.shape
    picks = expert_ids.shape[1]
    experts = lax.axis_size("dp") * lax.axis_size("expert")
    cores = lax.axis_size("tensor")
    hidden = w_gate.shape[2]
    per_core = min(3 * toks * picks // experts, toks) // cores
    per_a = 2 * per_core // 3
    per_b = per_core - per_a
    core = lax.axis_index("tensor")
    factor = 1.0 / (toks * picks) ** 0.5

    def swap(rows):
        return lax.ppermute(rows, "tensor", [(0, 1), (1, 0)])

    base_a = jnp.stack([core * per_core, core]).astype(jnp.int32)
    base_b = jnp.stack([core * per_core + per_a, core]).astype(jnp.int32)

    packed_a, pos, gm = route_pack(base_a, expert_ids.T, gates.T, tokens, experts, per_a)
    x_a = exchange(packed_a)
    packed_b = pack(base_b, pos, tokens, per_b)
    mats = jnp.concatenate([w_gate[0], w_up[0], v_gate[0], v_up[0]], axis=1)
    down_own = jnp.concatenate([v_down[0], w_down[0]], axis=0)
    down_other = swap(down_own)

    def run_forward(x_own):
        x_other = swap(x_own)
        mine = forward(x_own, mats, hidden)
        theirs = forward(x_other, mats, hidden)
        part = part_rows(mine[0], swap(theirs[0]), down_own, down_other)
        return part, (x_own, *mine), (x_other, *theirs)

    x_b = exchange(packed_b)
    part_a, mine_a, theirs_a = run_forward(x_a)
    ret_a = exchange(part_a)
    part_b, mine_b, theirs_b = run_forward(x_b)
    ret_b = exchange(part_b)
    own = combine(base_a, pos, gm, ret_a, None, per_a)
    own = combine(base_b, pos, gm, ret_b, own, per_b)
    other = swap(own)
    weight = token_weight[:, None]
    send_a, tangent = weigh_pack(base_a, pos, gm, weight, own, other, per_a, width // cores)
    q_a = exchange(send_a)
    (send_b,) = weigh_pack(base_b, pos, gm, weight, own, other, per_b, 0)
    q_b = exchange(send_b)
    down = w_down[0]
    sums = backward((q_a, *mine_a), (swap(q_a), *theirs_a), down, (), None)
    gv_gate, gv_up, gv_down = backward(
        (q_b, *mine_b), (swap(q_b), *theirs_b), down, sums, factor
    )
    return gv_gate, gv_up, gv_down, tangent


def solution(mesh):
    rows = P(GROUP, None)
    cols = P(GROUP, None, "tensor")
    down = P(GROUP, "tensor", None)
    in_specs = (rows, rows, rows, P(GROUP), cols, cols, down, cols, cols, down)
    out_specs = (cols, cols, down, P(GROUP, "tensor"))
    return jax.shard_map(body, mesh=mesh, in_specs=in_specs, out_specs=out_specs, check_vma=False)
```

```python
import jax
import jax.numpy as jnp
from jax import lax
from jax.experimental import pallas as pl
from jax.experimental.pallas import tpu as pltpu
from jax.sharding import PartitionSpec as P

BF = jnp.bfloat16
F32 = jnp.float32
GROUP = ("dp", "expert")
VMEM_LIMIT = 60 * 1024 * 1024
TILE = 256
PIECE = 256


def params():
    return pltpu.CompilerParams(
        dimension_semantics=("arbitrary",), vmem_limit_bytes=VMEM_LIMIT
    )


def cost(flops, nbytes):
    return pl.CostEstimate(flops=flops // 16, bytes_accessed=nbytes // 16, transcendentals=0)


def fixed(shape):
    return pl.BlockSpec(
        shape, lambda i: (0,) * len(shape), pipeline_mode=pl.Buffered(buffer_count=1)
    )


def smem():
    return pl.BlockSpec(memory_space=pltpu.SMEM)


def mm(left, right):
    return jnp.dot(left, right, preferred_element_type=F32)


def mm_t(left, right):
    return lax.dot_general(left, right, (((1,), (1,)), ((), ())), preferred_element_type=F32)


def mm_rows(left, right):
    return lax.dot_general(left, right, (((0,), (0,)), ((), ())), preferred_element_type=F32)


def spread(rows, per):
    count, toks = rows.shape
    return jnp.broadcast_to(rows[:, None, :], (count, per, toks)).reshape(count * per, toks)


def slot_match(pos, base, per):
    count, toks = pos.shape
    slot = lax.broadcasted_iota(jnp.int32, (count, per, toks), 1).reshape(count * per, toks)
    return spread(pos, per) == (slot + base).astype(F32)


def route_pack(base, ids_t, gates_t, tokens, experts, per):
    picks, toks = ids_t.shape
    width = tokens.shape[1]
    step = TILE // per
    steps = experts // step

    def kernel(base_ref, ids_ref, gates_ref, tok_ref, x_ref, pos_ref, gm_ref):
        i = pl.program_id(0)

        @pl.when(i == 0)
        def _():
            label = lax.broadcasted_iota(jnp.int32, (experts, toks), 0)
            hits = jnp.zeros((experts, toks), F32)
            gm = jnp.zeros((experts, toks), F32)
            for k in range(picks):
                match = ids_ref[k : k + 1, :] == label
                hits = jnp.where(match, 1.0, hits)
                gm = jnp.where(match, gates_ref[k : k + 1, :], gm)
            row = lax.broadcasted_iota(jnp.int32, (toks, toks), 0)
            col = lax.broadcasted_iota(jnp.int32, (toks, toks), 1)
            before = jnp.where(row < col, 1.0, 0.0).astype(BF)
            pos = mm(hits.astype(BF), before)
            pos_ref[...] = jnp.where(hits > 0.5, pos, -1.0)
            gm_ref[...] = gm

        pos = pos_ref[pl.ds(pl.multiple_of(i * step, step), step), :]
        hot = jnp.where(slot_match(pos, base_ref[0], per), 1.0, 0.0).astype(BF)
        x_ref[...] = mm(hot, tok_ref[...]).astype(BF)

    return pl.pallas_call(
        kernel,
        grid=(steps,),
        in_specs=[smem(), fixed((picks, toks)), fixed((picks, toks)), fixed((toks, width))],
        out_specs=[
            pl.BlockSpec((TILE, width), lambda i: (i, 0)),
            pl.BlockSpec((experts, toks), lambda i: (0, 0)),
            pl.BlockSpec((experts, toks), lambda i: (0, 0)),
        ],
        out_shape=[
            jax.ShapeDtypeStruct((experts * per, width), BF),
            jax.ShapeDtypeStruct((experts, toks), F32),
            jax.ShapeDtypeStruct((experts, toks), F32),
        ],
        compiler_params=params(),
        cost_estimate=cost(2 * experts * per * toks * width, 2 * experts * per * width),
        name="route_pack",
    )(base, ids_t, gates_t, tokens)


def pack(base, pos, tokens, per):
    experts, toks = pos.shape
    width = tokens.shape[1]
    step = TILE // per

    def kernel(base_ref, pos_ref, tok_ref, x_ref):
        hot = jnp.where(slot_match(pos_ref[...], base_ref[0], per), 1.0, 0.0).astype(BF)
        x_ref[...] = mm(hot, tok_ref[...]).astype(BF)

    return pl.pallas_call(
        kernel,
        grid=(experts // step,),
        in_specs=[smem(), pl.BlockSpec((step, toks), lambda i: (i, 0)), fixed((toks, width))],
        out_specs=pl.BlockSpec((TILE, width), lambda i: (i, 0)),
        out_shape=jax.ShapeDtypeStruct((experts * per, width), BF),
        compiler_params=params(),
        cost_estimate=cost(2 * experts * per * toks * width, 2 * experts * per * width),
        name="pack",
    )(base, pos, tokens)


def forward(rows, mats, hidden):
    count, width = rows.shape

    def kernel(x_ref, w_ref, ad_ref, silu_ref, us_ref):
        pre = mm(x_ref[...], w_ref[...])
        gate = pre[:, :hidden]
        up = pre[:, hidden : 2 * hidden]
        d_gate = pre[:, 2 * hidden : 3 * hidden]
        d_up = pre[:, 3 * hidden :]
        sigma = jax.nn.sigmoid(gate)
        silu = gate * sigma
        us = sigma * (1.0 + gate * (1.0 - sigma)) * up
        ad_ref[:, :hidden] = (silu * up).astype(BF)
        ad_ref[:, hidden:] = (us * d_gate + silu * d_up).astype(BF)
        silu_ref[...] = silu
        us_ref[...] = us

    return pl.pallas_call(
        kernel,
        grid=(count // TILE,),
        in_specs=[pl.BlockSpec((TILE, width), lambda i: (i, 0)), fixed((width, 4 * hidden))],
        out_specs=[
            pl.BlockSpec((TILE, 2 * hidden), lambda i: (i, 0)),
            pl.BlockSpec((TILE, hidden), lambda i: (i, 0)),
            pl.BlockSpec((TILE, hidden), lambda i: (i, 0)),
        ],
        out_shape=[
            jax.ShapeDtypeStruct((count, 2 * hidden), BF),
            jax.ShapeDtypeStruct((count, hidden), F32),
            jax.ShapeDtypeStruct((count, hidden), F32),
        ],
        compiler_params=params(),
        cost_estimate=cost(8 * count * width * hidden, 2 * count * width + 12 * count * hidden),
        name="forward",
    )(rows, mats)


def part_rows(ad_own, ad_other, down_own, down_other):
    count, inner = ad_own.shape
    width = down_own.shape[1]

    def kernel(a_ref, b_ref, wa_ref, wb_ref, out_ref):
        out_ref[...] = (mm(a_ref[...], wa_ref[...]) + mm(b_ref[...], wb_ref[...])).astype(BF)

    return pl.pallas_call(
        kernel,
        grid=(count // TILE,),
        in_specs=[
            pl.BlockSpec((TILE, inner), lambda i: (i, 0)),
            pl.BlockSpec((TILE, inner), lambda i: (i, 0)),
            fixed((inner, width)),
            fixed((inner, width)),
        ],
        out_specs=pl.BlockSpec((TILE, width), lambda i: (i, 0)),
        out_shape=jax.ShapeDtypeStruct((count, width), BF),
        compiler_params=params(),
        cost_estimate=cost(4 * count * width * inner, 2 * count * width + 4 * inner * width),
        name="part_rows",
    )(ad_own, ad_other, down_own, down_other)


def split_gates(pos, gm, base, per):
    weight = jnp.where(slot_match(pos, base, per), spread(gm, per), 0.0)
    high = weight.astype(BF)
    low = (weight - high.astype(F32)).astype(BF)
    return high, low


def combine(base, pos, gm, rows, start, per):
    experts, toks = pos.shape
    width = rows.shape[1]
    step = TILE // per
    steps = experts // step
    first = start is None

    def kernel(base_ref, pos_ref, gm_ref, rows_ref, *rest):
        start_ref = None if first else rest[0]
        out_ref, acc_ref = rest[-2:]
        i = pl.program_id(0)
        high, low = split_gates(pos_ref[...], gm_ref[...], base_ref[0], per)
        term = mm_rows(jnp.concatenate([high, low], axis=1), rows_ref[...])

        @pl.when(i == 0)
        def _():
            acc_ref[...] = term

        @pl.when(i > 0)
        def _():
            acc_ref[...] += term

        @pl.when(i == steps - 1)
        def _():
            total = acc_ref[:toks, :] + acc_ref[toks:, :]
            out_ref[...] = total if first else total + start_ref[...]

    extra = [] if first else [start]
    return pl.pallas_call(
        kernel,
        grid=(steps,),
        in_specs=[
            smem(),
            pl.BlockSpec((step, toks), lambda i: (i, 0)),
            pl.BlockSpec((step, toks), lambda i: (i, 0)),
            pl.BlockSpec((TILE, width), lambda i: (i, 0)),
        ]
        + [fixed((toks, width)) for _ in extra],
        out_specs=pl.BlockSpec((toks, width), lambda i: (0, 0)),
        out_shape=jax.ShapeDtypeStruct((toks, width), F32),
        scratch_shapes=[pltpu.VMEM((2 * toks, width), F32)],
        compiler_params=params(),
        cost_estimate=cost(4 * experts * per * toks * width, 2 * experts * per * width),
        name="combine",
    )(base, pos, gm, rows, *extra)


def weigh_pack(base, pos, gm, weight, own, other, per, half):
    experts, toks = pos.shape
    width = own.shape[1]
    step = TILE // per

    def kernel(base_ref, pos_ref, gm_ref, tw_ref, own_ref, other_ref, q_ref, *rest):
        split_ref = rest[-1]

        @pl.when(pl.program_id(0) == 0)
        def _():
            if half:
                cols = pl.ds(pl.multiple_of(base_ref[1] * half, half), half)
                rest[0][...] = (own_ref[:, cols] + other_ref[:, cols]).astype(BF)
            scaled = tw_ref[...] * (own_ref[...] + other_ref[...])
            high = scaled.astype(BF)
            split_ref[:toks, :] = high
            split_ref[toks:, :] = (scaled - high.astype(F32)).astype(BF)

        match = slot_match(pos_ref[...], base_ref[0], per)
        hot = jnp.where(match, 1.0, 0.0).astype(BF)
        gate = jnp.sum(jnp.where(match, spread(gm_ref[...], per), 0.0), axis=1, keepdims=True)
        row = mm(jnp.concatenate([hot, hot], axis=1), split_ref[...])
        q_ref[...] = (gate * row).astype(BF)

    out_specs = [pl.BlockSpec((TILE, width), lambda i: (i, 0))]
    out_shape = [jax.ShapeDtypeStruct((experts * per, width), BF)]
    if half:
        out_specs.append(pl.BlockSpec((toks, half), lambda i: (0, 0)))
        out_shape.append(jax.ShapeDtypeStruct((toks, half), BF))
    return pl.pallas_call(
        kernel,
        grid=(experts // step,),
        in_specs=[
            smem(),
            pl.BlockSpec((step, toks), lambda i: (i, 0)),
            pl.BlockSpec((step, toks), lambda i: (i, 0)),
            fixed((toks, 1)),
            fixed((toks, width)),
            fixed((toks, width)),
        ],
        out_specs=out_specs,
        out_shape=out_shape,
        scratch_shapes=[pltpu.VMEM((2 * toks, width), BF)],
        compiler_params=params(),
        cost_estimate=cost(6 * experts * per * toks * width, 2 * experts * per * width),
        name="weigh_pack",
    )(base, pos, gm, weight, own, other)


def gradients(q, silu, us, down):
    count, width = q.shape
    hidden = down.shape[0]
    tile = min(TILE, count)

    def kernel(q_ref, silu_ref, us_ref, down_ref, g_ref):
        back = mm_t(q_ref[...], down_ref[...])
        g_ref[:, :hidden] = (back * us_ref[...]).astype(BF)
        g_ref[:, hidden:] = (back * silu_ref[...]).astype(BF)

    return pl.pallas_call(
        kernel,
        grid=(count // tile,),
        in_specs=[
            pl.BlockSpec((tile, width), lambda i: (i, 0)),
            pl.BlockSpec((tile, hidden), lambda i: (i, 0)),
            pl.BlockSpec((tile, hidden), lambda i: (i, 0)),
            fixed((hidden, width)),
        ],
        out_specs=pl.BlockSpec((tile, 2 * hidden), lambda i: (i, 0)),
        out_shape=jax.ShapeDtypeStruct((count, 2 * hidden), BF),
        compiler_params=params(),
        cost_estimate=cost(2 * count * width * hidden, 2 * count * width),
        name="gradients",
    )(q, silu, us, down)


def outer_sums(own, other, start, factor, hidden):
    count, width = own[0].shape
    piece = PIECE

    def kernel(*refs):
        gate_out, up_out, down_out = refs[-3:]
        gate_up, down = 0.0, 0.0
        for q_ref, x_ref, g_ref, act_ref in (refs[:4], refs[4:8]):
            gate_up += mm_rows(x_ref[...], g_ref[...])
            down += mm_rows(act_ref[...], q_ref[...])
        terms = [gate_up[:, :hidden], gate_up[:, hidden:], down]
        for out, term, begin in zip((gate_out, up_out, down_out), terms, refs[8:11] if start else [None] * 3):
            out[0] = factor * term + begin[0] if start else factor * term

    def specs():
        return [
            pl.BlockSpec((count, piece), lambda i: (0, i)),
            pl.BlockSpec((count, piece), lambda i: (0, i)),
            fixed((count, 2 * hidden)),
            pl.BlockSpec(
                (count, hidden), lambda i: (0, 0), pipeline_mode=pl.Buffered(buffer_count=1)
            ),
        ]

    def results():
        return [
            pl.BlockSpec((1, piece, hidden), lambda i: (0, i, 0)),
            pl.BlockSpec((1, piece, hidden), lambda i: (0, i, 0)),
            pl.BlockSpec((1, hidden, piece), lambda i: (0, 0, i)),
        ]

    shapes = [(1, width, hidden), (1, width, hidden), (1, hidden, width)]
    return pl.pallas_call(
        kernel,
        grid=(width // piece,),
        in_specs=specs() + specs() + (results() if start else []),
        out_specs=results(),
        out_shape=[jax.ShapeDtypeStruct(shape, F32) for shape in shapes],
        compiler_params=params(),
        cost_estimate=cost(12 * count * width * hidden, 8 * count * width),
        name="outer_sums",
    )(*own, *other, *start)


def exchange(rows):
    return lax.all_to_all(rows, GROUP, split_axis=0, concat_axis=0, tiled=True)


def body(tokens, expert_ids, gates, token_weight, w_gate, w_up, w_down, v_gate, v_up, v_down):
    toks, width = tokens.shape
    picks = expert_ids.shape[1]
    experts = lax.axis_size("dp") * lax.axis_size("expert")
    cores = lax.axis_size("tensor")
    hidden = w_gate.shape[2]
    per_core = min(3 * toks * picks // experts, toks) // cores
    per_a = 2 * per_core // 3
    per_b = per_core - per_a
    core = lax.axis_index("tensor")
    factor = 1.0 / (toks * picks) ** 0.5

    def swap(rows):
        return lax.ppermute(rows, "tensor", [(0, 1), (1, 0)])

    base_a = jnp.stack([core * per_core, core]).astype(jnp.int32)
    base_b = jnp.stack([core * per_core + per_a, core]).astype(jnp.int32)

    packed_a, pos, gm = route_pack(base_a, expert_ids.T, gates.T, tokens, experts, per_a)
    x_a = exchange(packed_a)
    packed_b = pack(base_b, pos, tokens, per_b)
    mats = jnp.concatenate([w_gate[0], w_up[0], v_gate[0], v_up[0]], axis=1)
    down_own = jnp.concatenate([v_down[0], w_down[0]], axis=0)
    x_a, packed_b, mats, down_own = lax.optimization_barrier((x_a, packed_b, mats, down_own))
    x_b = exchange(packed_b)
    down_other = swap(down_own)

    def run_forward(x_own):
        x_other = swap(x_own)
        mine = forward(x_own, mats, hidden)
        theirs = forward(x_other, mats, hidden)
        part = part_rows(mine[0], swap(theirs[0]), down_own, down_other)
        return part, (x_own, *mine), (x_other, *theirs)

    part_a, mine_a, theirs_a = run_forward(x_a)
    x_b, part_a = lax.optimization_barrier((x_b, part_a))
    ret_a = exchange(part_a)
    part_b, mine_b, theirs_b = run_forward(x_b)
    ret_a, part_b = lax.optimization_barrier((ret_a, part_b))
    ret_b = exchange(part_b)
    own = combine(base_a, pos, gm, ret_a, None, per_a)
    ret_b, own = lax.optimization_barrier((ret_b, own))
    own = combine(base_b, pos, gm, ret_b, own, per_b)
    other = swap(own)
    weight = token_weight[:, None]
    send_a, tangent = weigh_pack(base_a, pos, gm, weight, own, other, per_a, width // cores)
    q_a = exchange(send_a)
    (send_b,) = weigh_pack(base_b, pos, gm, weight, own, other, per_b, 0)
    q_a, send_b = lax.optimization_barrier((q_a, send_b))
    q_b = exchange(send_b)
    down = w_down[0]

    def run_backward(q_own, mine, theirs, start):
        q_other = swap(q_own)
        sides = []
        for q, (x, ad, silu, us) in ((q_own, mine), (q_other, theirs)):
            sides.append((q, x, gradients(q, silu, us, down), ad))
        return outer_sums(*sides, start, factor, hidden)

    sums = run_backward(q_a, mine_a, theirs_a, ())
    q_b, sums = lax.optimization_barrier((q_b, sums))
    gv_gate, gv_up, gv_down = run_backward(q_b, mine_b, theirs_b, sums)
    return gv_gate, gv_up, gv_down, tangent


def solution(mesh):
    rows = P(GROUP, None)
    cols = P(GROUP, None, "tensor")
    down = P(GROUP, "tensor", None)
    in_specs = (rows, rows, rows, P(GROUP), cols, cols, down, cols, cols, down)
    out_specs = (cols, cols, down, P(GROUP, "tensor"))
    return jax.shard_map(body, mesh=mesh, in_specs=in_specs, out_specs=out_specs, check_vma=False)
```

```python
import jax
import jax.numpy as jnp
from jax import lax
from jax.experimental import pallas as pl
from jax.experimental.pallas import tpu as pltpu
from jax.sharding import PartitionSpec as P

BF = jnp.bfloat16
F32 = jnp.float32
GROUP = ("dp", "expert")
VMEM_LIMIT = 63 * 1024 * 1024
TILE = 256
PIECE = 512
LAST_PIECE = 512
ROWS = 512
SLOTS = (1, 2)


def params():
    return pltpu.CompilerParams(
        dimension_semantics=("arbitrary",), vmem_limit_bytes=VMEM_LIMIT
    )


def cost(flops, nbytes):
    return pl.CostEstimate(flops=flops // 16, bytes_accessed=nbytes // 16, transcendentals=0)


def fixed(shape):
    return pl.BlockSpec(
        shape, lambda i: (0,) * len(shape), pipeline_mode=pl.Buffered(buffer_count=1)
    )


def smem():
    return pl.BlockSpec(memory_space=pltpu.SMEM)


def mm(left, right):
    return jnp.dot(left, right, preferred_element_type=F32)


def mm_t(left, right):
    return lax.dot_general(left, right, (((1,), (1,)), ((), ())), preferred_element_type=F32)


def mm_rows(left, right):
    return lax.dot_general(left, right, (((0,), (0,)), ((), ())), preferred_element_type=F32)


def spread(rows, per):
    count, toks = rows.shape
    return jnp.broadcast_to(rows[:, None, :], (count, per, toks)).reshape(count * per, toks)


def slot_match(pos, base, per):
    count, toks = pos.shape
    slot = lax.broadcasted_iota(jnp.int32, (count, per, toks), 1).reshape(count * per, toks)
    return spread(pos, per) == (slot + base).astype(F32)


def route_pack(base, ids_t, gates_t, tokens, experts, per):
    picks, toks = ids_t.shape
    width = tokens.shape[1]
    step = TILE // per
    steps = experts // step

    def kernel(base_ref, ids_ref, gates_ref, tok_ref, x_ref, pos_ref, gm_ref):
        i = pl.program_id(0)

        @pl.when(i == 0)
        def _():
            label = lax.broadcasted_iota(jnp.int32, (experts, toks), 0)
            hits = jnp.zeros((experts, toks), F32)
            gm = jnp.zeros((experts, toks), F32)
            for k in range(picks):
                match = ids_ref[k : k + 1, :] == label
                hits = jnp.where(match, 1.0, hits)
                gm = jnp.where(match, gates_ref[k : k + 1, :], gm)
            row = lax.broadcasted_iota(jnp.int32, (toks, toks), 0)
            col = lax.broadcasted_iota(jnp.int32, (toks, toks), 1)
            before = jnp.where(row < col, 1.0, 0.0).astype(BF)
            pos = mm(hits.astype(BF), before)
            pos_ref[...] = jnp.where(hits > 0.5, pos, -1.0)
            gm_ref[...] = gm

        pos = pos_ref[pl.ds(pl.multiple_of(i * step, step), step), :]
        hot = jnp.where(slot_match(pos, base_ref[0], per), 1.0, 0.0).astype(BF)
        x_ref[...] = mm(hot, tok_ref[...]).astype(BF)

    return pl.pallas_call(
        kernel,
        grid=(steps,),
        in_specs=[smem(), fixed((picks, toks)), fixed((picks, toks)), fixed((toks, width))],
        out_specs=[
            pl.BlockSpec((TILE, width), lambda i: (i, 0)),
            pl.BlockSpec((experts, toks), lambda i: (0, 0)),
            pl.BlockSpec((experts, toks), lambda i: (0, 0)),
        ],
        out_shape=[
            jax.ShapeDtypeStruct((experts * per, width), BF),
            jax.ShapeDtypeStruct((experts, toks), F32),
            jax.ShapeDtypeStruct((experts, toks), F32),
        ],
        compiler_params=params(),
        cost_estimate=cost(2 * experts * per * toks * width, 2 * experts * per * width),
        name="route_pack",
    )(base, ids_t, gates_t, tokens)


def pack(base, pos, tokens, per):
    experts, toks = pos.shape
    width = tokens.shape[1]
    step = TILE // per

    def kernel(base_ref, pos_ref, tok_ref, x_ref):
        hot = jnp.where(slot_match(pos_ref[...], base_ref[0], per), 1.0, 0.0).astype(BF)
        x_ref[...] = mm(hot, tok_ref[...]).astype(BF)

    return pl.pallas_call(
        kernel,
        grid=(experts // step,),
        in_specs=[smem(), pl.BlockSpec((step, toks), lambda i: (i, 0)), fixed((toks, width))],
        out_specs=pl.BlockSpec((TILE, width), lambda i: (i, 0)),
        out_shape=jax.ShapeDtypeStruct((experts * per, width), BF),
        compiler_params=params(),
        cost_estimate=cost(2 * experts * per * toks * width, 2 * experts * per * width),
        name="pack",
    )(base, pos, tokens)


def forward(rows, mats, hidden):
    count, width = rows.shape

    def kernel(x_ref, w_ref, ad_ref, silu_ref, us_ref):
        pre = mm(x_ref[...], w_ref[...])
        gate = pre[:, :hidden]
        up = pre[:, hidden : 2 * hidden]
        d_gate = pre[:, 2 * hidden : 3 * hidden]
        d_up = pre[:, 3 * hidden :]
        sigma = jax.nn.sigmoid(gate)
        silu = gate * sigma
        us = sigma * (1.0 + gate * (1.0 - sigma)) * up
        ad_ref[:, :hidden] = (silu * up).astype(BF)
        ad_ref[:, hidden:] = (us * d_gate + silu * d_up).astype(BF)
        silu_ref[...] = silu.astype(BF)
        us_ref[...] = us.astype(BF)

    return pl.pallas_call(
        kernel,
        grid=(count // TILE,),
        in_specs=[pl.BlockSpec((TILE, width), lambda i: (i, 0)), fixed((width, 4 * hidden))],
        out_specs=[
            pl.BlockSpec((TILE, 2 * hidden), lambda i: (i, 0)),
            pl.BlockSpec((TILE, hidden), lambda i: (i, 0)),
            pl.BlockSpec((TILE, hidden), lambda i: (i, 0)),
        ],
        out_shape=[
            jax.ShapeDtypeStruct((count, 2 * hidden), BF),
            jax.ShapeDtypeStruct((count, hidden), BF),
            jax.ShapeDtypeStruct((count, hidden), BF),
        ],
        compiler_params=params(),
        cost_estimate=cost(8 * count * width * hidden, 2 * count * width + 12 * count * hidden),
        name="forward",
    )(rows, mats)


def part_rows(ad_own, ad_other, down_own, down_other):
    count, inner = ad_own.shape
    width = down_own.shape[1]

    def kernel(a_ref, b_ref, wa_ref, wb_ref, out_ref):
        out_ref[...] = (mm(a_ref[...], wa_ref[...]) + mm(b_ref[...], wb_ref[...])).astype(BF)

    return pl.pallas_call(
        kernel,
        grid=(count // TILE,),
        in_specs=[
            pl.BlockSpec((TILE, inner), lambda i: (i, 0)),
            pl.BlockSpec((TILE, inner), lambda i: (i, 0)),
            fixed((inner, width)),
            fixed((inner, width)),
        ],
        out_specs=pl.BlockSpec((TILE, width), lambda i: (i, 0)),
        out_shape=jax.ShapeDtypeStruct((count, width), BF),
        compiler_params=params(),
        cost_estimate=cost(4 * count * width * inner, 2 * count * width + 4 * inner * width),
        name="part_rows",
    )(ad_own, ad_other, down_own, down_other)


def gate_matrix(base, pos, gm, per):
    experts, toks = pos.shape
    step = TILE // per

    def kernel(base_ref, pos_ref, gm_ref, out_ref):
        match = slot_match(pos_ref[...], base_ref[0], per)
        weight = jnp.where(match, spread(gm_ref[...], per), 0.0).T
        high = weight.astype(BF)
        out_ref[:toks, :] = high
        out_ref[toks:, :] = (weight - high.astype(F32)).astype(BF)

    return pl.pallas_call(
        kernel,
        grid=(experts // step,),
        in_specs=[
            smem(),
            pl.BlockSpec((step, toks), lambda i: (i, 0)),
            pl.BlockSpec((step, toks), lambda i: (i, 0)),
        ],
        out_specs=pl.BlockSpec((2 * toks, TILE), lambda i: (0, i)),
        out_shape=jax.ShapeDtypeStruct((2 * toks, experts * per), BF),
        compiler_params=params(),
        cost_estimate=cost(4 * experts * per * toks, 4 * experts * per * toks),
        name="gate_matrix",
    )(base, pos, gm)


def combine(matrix, rows, start):
    count, width = rows.shape
    toks = matrix.shape[0] // 2
    piece = 1024

    def kernel(matrix_ref, rows_ref, *rest):
        both = mm(matrix_ref[...], rows_ref[...])
        total = both[:toks] + both[toks:]
        rest[-1][...] = total if start is None else total + rest[0][...]

    extra = [] if start is None else [start]
    column = pl.BlockSpec((toks, piece), lambda i: (0, i))
    return pl.pallas_call(
        kernel,
        grid=(width // piece,),
        in_specs=[fixed((2 * toks, count)), pl.BlockSpec((count, piece), lambda i: (0, i))]
        + [column for _ in extra],
        out_specs=column,
        out_shape=jax.ShapeDtypeStruct((toks, width), F32),
        compiler_params=params(),
        cost_estimate=cost(4 * count * toks * width, 2 * count * width),
        name="combine",
    )(matrix, rows, *extra)


def weigh_pack(base, pos, gm, weight, own, other, per, half):
    experts, toks = pos.shape
    width = own.shape[1]
    step = TILE // per

    def kernel(base_ref, pos_ref, gm_ref, tw_ref, own_ref, other_ref, q_ref, *rest):
        split_ref = rest[-1]

        @pl.when(pl.program_id(0) == 0)
        def _():
            if half:
                cols = pl.ds(pl.multiple_of(base_ref[1] * half, half), half)
                rest[0][...] = (own_ref[:, cols] + other_ref[:, cols]).astype(BF)
            scaled = tw_ref[...] * (own_ref[...] + other_ref[...])
            high = scaled.astype(BF)
            split_ref[:toks, :] = high
            split_ref[toks:, :] = (scaled - high.astype(F32)).astype(BF)

        match = slot_match(pos_ref[...], base_ref[0], per)
        hot = jnp.where(match, 1.0, 0.0).astype(BF)
        gate = jnp.sum(jnp.where(match, spread(gm_ref[...], per), 0.0), axis=1, keepdims=True)
        row = mm(jnp.concatenate([hot, hot], axis=1), split_ref[...])
        q_ref[...] = (gate * row).astype(BF)

    out_specs = [pl.BlockSpec((TILE, width), lambda i: (i, 0))]
    out_shape = [jax.ShapeDtypeStruct((experts * per, width), BF)]
    if half:
        out_specs.append(pl.BlockSpec((toks, half), lambda i: (0, 0)))
        out_shape.append(jax.ShapeDtypeStruct((toks, half), BF))
    return pl.pallas_call(
        kernel,
        grid=(experts // step,),
        in_specs=[
            smem(),
            pl.BlockSpec((step, toks), lambda i: (i, 0)),
            pl.BlockSpec((step, toks), lambda i: (i, 0)),
            fixed((toks, 1)),
            fixed((toks, width)),
            fixed((toks, width)),
        ],
        out_specs=out_specs,
        out_shape=out_shape,
        scratch_shapes=[pltpu.VMEM((2 * toks, width), BF)],
        compiler_params=params(),
        cost_estimate=cost(6 * experts * per * toks * width, 2 * experts * per * width),
        name="weigh_pack",
    )(base, pos, gm, weight, own, other)


def gradients(q, silu, us, down):
    count, width = q.shape
    hidden = down.shape[0]
    tile = min(TILE, count)

    def kernel(q_ref, silu_ref, us_ref, down_ref, g_ref):
        back = mm_t(q_ref[...], down_ref[...])
        g_ref[:, :hidden] = (back * us_ref[...]).astype(BF)
        g_ref[:, hidden:] = (back * silu_ref[...]).astype(BF)

    return pl.pallas_call(
        kernel,
        grid=(count // tile,),
        in_specs=[
            pl.BlockSpec((tile, width), lambda i: (i, 0)),
            pl.BlockSpec((tile, hidden), lambda i: (i, 0)),
            pl.BlockSpec((tile, hidden), lambda i: (i, 0)),
            fixed((hidden, width)),
        ],
        out_specs=pl.BlockSpec((tile, 2 * hidden), lambda i: (i, 0)),
        out_shape=jax.ShapeDtypeStruct((count, 2 * hidden), BF),
        compiler_params=params(),
        cost_estimate=cost(2 * count * width * hidden, 2 * count * width),
        name="gradients",
    )(q, silu, us, down)


def phased_sums(own, other, down, factor):
    count, width = own[0].shape
    hidden = down.shape[0]
    tile = min(ROWS, count)
    piece = PIECE
    tiles = count // tile
    head = 2 * tiles

    def kernel(*refs):
        sides = (refs[:5], refs[5:10])
        down_ref = refs[10]
        outs = refs[11:14]
        g_ref, turned_ref, q_ref = refs[14:]
        i = pl.program_id(0)

        for side, (tile_ref, _, ad_ref, silu_ref, us_ref) in enumerate(sides):
            for n in range(tiles):

                @pl.when(i == side * tiles + n)
                def _(side=side, n=n, tile_ref=tile_ref, ad_ref=ad_ref, silu_ref=silu_ref, us_ref=us_ref):
                    rows = slice(side * count + n * tile, side * count + (n + 1) * tile)
                    q = tile_ref[...]
                    back = mm_t(q, down_ref[...])
                    g_ref[rows, :hidden] = (back * us_ref[...]).astype(BF)
                    g_ref[rows, hidden:] = (back * silu_ref[...]).astype(BF)
                    turned_ref[:, rows] = ad_ref[...].T
                    q_ref[rows, :] = q

        @pl.when(i >= head)
        def _():
            cols = pl.ds(pl.multiple_of(jnp.maximum(i - head, 0) * piece, piece), piece)
            gate_up = mm_rows(sides[0][1][...], g_ref[:count, :])
            gate_up += mm_rows(sides[1][1][...], g_ref[count:, :])
            outs[0][0] = factor * gate_up[:, :hidden]
            outs[1][0] = factor * gate_up[:, hidden:]
            outs[2][0] = factor * mm(turned_ref[...], q_ref[:, cols])

    def later(i):
        return jnp.maximum(i - head, 0)

    def specs(first):
        def at(i):
            return jnp.clip(i - first, 0, tiles - 1)

        return [
            pl.BlockSpec((tile, width), lambda i: (at(i), 0)),
            pl.BlockSpec((count, piece), lambda i: (0, later(i))),
            pl.BlockSpec((tile, hidden), lambda i: (at(i), 0)),
            pl.BlockSpec((tile, hidden), lambda i: (at(i), 0)),
            pl.BlockSpec((tile, hidden), lambda i: (at(i), 0)),
        ]

    shapes = [(1, width, hidden), (1, width, hidden), (1, hidden, width)]
    return pl.pallas_call(
        kernel,
        grid=(head + width // piece,),
        in_specs=specs(0) + specs(tiles) + [fixed((hidden, width))],
        out_specs=[
            pl.BlockSpec((1, piece, hidden), lambda i: (0, later(i), 0)),
            pl.BlockSpec((1, piece, hidden), lambda i: (0, later(i), 0)),
            pl.BlockSpec((1, hidden, piece), lambda i: (0, 0, later(i))),
        ],
        out_shape=[jax.ShapeDtypeStruct(shape, F32) for shape in shapes],
        scratch_shapes=[
            pltpu.VMEM((2 * count, 2 * hidden), BF),
            pltpu.VMEM((hidden, 2 * count), BF),
            pltpu.VMEM((2 * count, width), BF),
        ],
        compiler_params=params(),
        cost_estimate=cost(16 * count * width * hidden, 8 * count * width),
        name="phased_sums",
    )(*own, *other, down)


def last_sums(own, other, silu, us, down, start, factor):
    count, width = own[0].shape
    hidden = down.shape[0]
    piece = LAST_PIECE

    def kernel(*refs):
        q_ref, x_ref, g_ref, act_ref, q2_ref, x2_ref, act2_ref, silu_ref, us_ref, down_ref = refs[:10]
        begins, outs = refs[10:13], refs[13:16]
        g2_ref, turned_ref = refs[16:]
        i = pl.program_id(0)

        @pl.when(i == 0)
        def _():
            back = mm_t(q2_ref[...], down_ref[...])
            g2_ref[:, :hidden] = (back * us_ref[...]).astype(BF)
            g2_ref[:, hidden:] = (back * silu_ref[...]).astype(BF)
            turned_ref[:, :count] = act_ref[...].T
            turned_ref[:, count:] = act2_ref[...].T

        cols = pl.ds(pl.multiple_of(i * piece, piece), piece)
        gate_up = mm_rows(x_ref[...], g_ref[...]) + mm_rows(x2_ref[...], g2_ref[...])
        below = mm(turned_ref[:, :count], q_ref[...]) + mm(turned_ref[:, count:], q2_ref[:, cols])
        terms = (gate_up[:, :hidden], gate_up[:, hidden:], below)
        for out, term, begin in zip(outs, terms, begins):
            out[0] = factor * term + begin[0]

    column = pl.BlockSpec((count, piece), lambda i: (0, i))
    act = pl.BlockSpec((count, hidden), lambda i: (0, 0), pipeline_mode=pl.Buffered(buffer_count=1))
    results = [
        pl.BlockSpec((1, piece, hidden), lambda i: (0, i, 0)),
        pl.BlockSpec((1, piece, hidden), lambda i: (0, i, 0)),
        pl.BlockSpec((1, hidden, piece), lambda i: (0, 0, i)),
    ]
    shapes = [(1, width, hidden), (1, width, hidden), (1, hidden, width)]
    return pl.pallas_call(
        kernel,
        grid=(width // piece,),
        in_specs=[column, column, fixed((count, 2 * hidden)), act]
        + [fixed((count, width)), column, act]
        + [fixed((count, hidden)), fixed((count, hidden)), fixed((hidden, width))]
        + results,
        out_specs=results,
        out_shape=[jax.ShapeDtypeStruct(shape, F32) for shape in shapes],
        scratch_shapes=[
            pltpu.VMEM((count, 2 * hidden), BF),
            pltpu.VMEM((hidden, 2 * count), BF),
        ],
        compiler_params=params(),
        cost_estimate=cost(14 * count * width * hidden, 8 * count * width),
        name="last_sums",
    )(*own, *other, silu, us, down, *start)


def exchange(rows):
    return lax.all_to_all(rows, GROUP, split_axis=0, concat_axis=0, tiled=True)


def body(tokens, expert_ids, gates, token_weight, w_gate, w_up, w_down, v_gate, v_up, v_down):
    toks, width = tokens.shape
    picks = expert_ids.shape[1]
    experts = lax.axis_size("dp") * lax.axis_size("expert")
    cores = lax.axis_size("tensor")
    hidden = w_gate.shape[2]
    per_core = min(3 * toks * picks // experts, toks) // cores
    core = lax.axis_index("tensor")
    factor = 1.0 / (toks * picks) ** 0.5

    def swap(rows):
        return lax.ppermute(rows, "tensor", [(0, 1), (1, 0)])

    chunks = []
    start = 0
    for per in SLOTS:
        size = per * per_core // sum(SLOTS)
        chunks.append((jnp.stack([core * per_core + start, core]).astype(jnp.int32), size))
        start += size
    count = len(chunks)

    base, per = chunks[0]
    packed, pos, gm = route_pack(base, expert_ids.T, gates.T, tokens, experts, per)
    arrived = exchange(packed)
    later = [pack(base, pos, tokens, per) for base, per in chunks[1:]]
    mats = jnp.concatenate([w_gate[0], w_up[0], v_gate[0], v_up[0]], axis=1)
    down_own = jnp.concatenate([v_down[0], w_down[0]], axis=0)
    matrices = [gate_matrix(base, pos, gm, per) for base, per in chunks]
    arrived, later, mats, down_own, matrices, weight = lax.optimization_barrier(
        (arrived, later, mats, down_own, matrices, token_weight[:, None])
    )
    down_other = swap(down_own)

    def run_forward(x_own):
        x_other = swap(x_own)
        mine = forward(x_own, mats, hidden)
        theirs = forward(x_other, mats, hidden)
        part = part_rows(mine[0], swap(theirs[0]), down_own, down_other)
        return part, (x_own, *mine), (x_other, *theirs)

    own, returned, sides = None, None, []
    for n in range(count):
        coming = exchange(later[n]) if n + 1 < count else returned
        part, mine, theirs = run_forward(arrived)
        sides.append((mine, theirs))
        if coming is not None:
            coming, part = lax.optimization_barrier((coming, part))
        if n + 1 < count:
            arrived = coming
            returned = exchange(part)
    if count > 1:
        own = combine(matrices[0], returned, None)
    last = exchange(part)
    if count > 1:
        last, own = lax.optimization_barrier((last, own))
    own = combine(matrices[-1], last, own)
    other = swap(own)
    order = sorted(range(count), key=lambda n: -chunks[n][1])

    base, per = chunks[order[0]]
    send, tangent = weigh_pack(base, pos, gm, weight, own, other, per, width // cores)
    q = exchange(send)
    if count > 1:
        base, per = chunks[order[1]]
        (send,) = weigh_pack(base, pos, gm, weight, own, other, per, 0)
        q, send = lax.optimization_barrier((q, send))
        q_next = exchange(send)
    down = w_down[0]

    mine, theirs = sides[order[0]]
    sums = phased_sums((q, *mine), (swap(q), *theirs), down, factor)
    if count > 1:
        q_next, sums = lax.optimization_barrier((q_next, sums))
        mine, theirs = sides[order[1]]
        q_other = swap(q_next)
        x, ad, silu, us = mine
        own_side = (q_next, x, gradients(q_next, silu, us, down), ad)
        x, ad, silu, us = theirs
        sums = last_sums(own_side, (q_other, x, ad), silu, us, down, sums, factor)
    gv_gate, gv_up, gv_down = sums
    return gv_gate, gv_up, gv_down, tangent


def solution(mesh):
    rows = P(GROUP, None)
    cols = P(GROUP, None, "tensor")
    down = P(GROUP, "tensor", None)
    in_specs = (rows, rows, rows, P(GROUP), cols, cols, down, cols, cols, down)
    out_specs = (cols, cols, down, P(GROUP, "tensor"))
    return jax.shard_map(body, mesh=mesh, in_specs=in_specs, out_specs=out_specs, check_vma=False)
```

```python
import jax
import jax.numpy as jnp
from jax import lax
from jax.experimental import pallas as pl
from jax.experimental.pallas import tpu as pltpu
from jax.sharding import PartitionSpec as P

BF = jnp.bfloat16
F32 = jnp.float32
GROUP = ("dp", "expert")
VMEM_LIMIT = 63 * 1024 * 1024
TILE = 256
PIECE = 512
LAST_PIECE = 1024
ROWS = 512
SLOTS = (1, 2)
COMBINE = 1024
WEIGH = 512


def params():
    return pltpu.CompilerParams(
        dimension_semantics=("arbitrary",), vmem_limit_bytes=VMEM_LIMIT
    )


def cost(flops, nbytes):
    return pl.CostEstimate(flops=flops // 16, bytes_accessed=nbytes // 16, transcendentals=0)


def fixed(shape):
    return pl.BlockSpec(
        shape, lambda i: (0,) * len(shape), pipeline_mode=pl.Buffered(buffer_count=1)
    )


def smem():
    return pl.BlockSpec(memory_space=pltpu.SMEM)


def mm(left, right):
    return jnp.dot(left, right, preferred_element_type=F32)


def mm_t(left, right):
    return lax.dot_general(left, right, (((1,), (1,)), ((), ())), preferred_element_type=F32)


def mm_rows(left, right):
    return lax.dot_general(left, right, (((0,), (0,)), ((), ())), preferred_element_type=F32)


def spread(rows, per):
    count, toks = rows.shape
    return jnp.broadcast_to(rows[:, None, :], (count, per, toks)).reshape(count * per, toks)


def slot_match(pos, base, per):
    count, toks = pos.shape
    slot = lax.broadcasted_iota(jnp.int32, (count, per, toks), 1).reshape(count * per, toks)
    return spread(pos, per) == (slot + base).astype(F32)


def route_pack(base, ids_t, gates_t, tokens, experts, per):
    picks, toks = ids_t.shape
    width = tokens.shape[1]
    step = TILE // per
    steps = experts // step

    def kernel(base_ref, ids_ref, gates_ref, tok_ref, x_ref, pos_ref, gm_ref):
        i = pl.program_id(0)

        @pl.when(i == 0)
        def _():
            label = lax.broadcasted_iota(jnp.int32, (experts, toks), 0)
            hits = jnp.zeros((experts, toks), F32)
            gm = jnp.zeros((experts, toks), F32)
            for k in range(picks):
                match = ids_ref[k : k + 1, :] == label
                hits = jnp.where(match, 1.0, hits)
                gm = jnp.where(match, gates_ref[k : k + 1, :], gm)
            row = lax.broadcasted_iota(jnp.int32, (toks, toks), 0)
            col = lax.broadcasted_iota(jnp.int32, (toks, toks), 1)
            before = jnp.where(row < col, 1.0, 0.0).astype(BF)
            pos = mm(hits.astype(BF), before)
            pos_ref[...] = jnp.where(hits > 0.5, pos, -1.0)
            gm_ref[...] = gm

        pos = pos_ref[pl.ds(pl.multiple_of(i * step, step), step), :]
        hot = jnp.where(slot_match(pos, base_ref[0], per), 1.0, 0.0).astype(BF)
        x_ref[...] = mm(hot, tok_ref[...]).astype(BF)

    return pl.pallas_call(
        kernel,
        grid=(steps,),
        in_specs=[smem(), fixed((picks, toks)), fixed((picks, toks)), fixed((toks, width))],
        out_specs=[
            pl.BlockSpec((TILE, width), lambda i: (i, 0)),
            pl.BlockSpec((experts, toks), lambda i: (0, 0)),
            pl.BlockSpec((experts, toks), lambda i: (0, 0)),
        ],
        out_shape=[
            jax.ShapeDtypeStruct((experts * per, width), BF),
            jax.ShapeDtypeStruct((experts, toks), F32),
            jax.ShapeDtypeStruct((experts, toks), F32),
        ],
        compiler_params=params(),
        cost_estimate=cost(2 * experts * per * toks * width, 2 * experts * per * width),
        name="route_pack",
    )(base, ids_t, gates_t, tokens)


def pack(base, pos, tokens, per):
    experts, toks = pos.shape
    width = tokens.shape[1]
    step = TILE // per

    def kernel(base_ref, pos_ref, tok_ref, x_ref):
        hot = jnp.where(slot_match(pos_ref[...], base_ref[0], per), 1.0, 0.0).astype(BF)
        x_ref[...] = mm(hot, tok_ref[...]).astype(BF)

    return pl.pallas_call(
        kernel,
        grid=(experts // step,),
        in_specs=[smem(), pl.BlockSpec((step, toks), lambda i: (i, 0)), fixed((toks, width))],
        out_specs=pl.BlockSpec((TILE, width), lambda i: (i, 0)),
        out_shape=jax.ShapeDtypeStruct((experts * per, width), BF),
        compiler_params=params(),
        cost_estimate=cost(2 * experts * per * toks * width, 2 * experts * per * width),
        name="pack",
    )(base, pos, tokens)


def forward(rows, mats, hidden):
    count, width = rows.shape

    def kernel(x_ref, w_ref, ad_ref, silu_ref, us_ref):
        pre = mm(x_ref[...], w_ref[...])
        gate = pre[:, :hidden]
        up = pre[:, hidden : 2 * hidden]
        d_gate = pre[:, 2 * hidden : 3 * hidden]
        d_up = pre[:, 3 * hidden :]
        sigma = jax.nn.sigmoid(gate)
        silu = gate * sigma
        us = sigma * (1.0 + gate * (1.0 - sigma)) * up
        ad_ref[:, :hidden] = (silu * up).astype(BF)
        ad_ref[:, hidden:] = (us * d_gate + silu * d_up).astype(BF)
        silu_ref[...] = silu.astype(BF)
        us_ref[...] = us.astype(BF)

    return pl.pallas_call(
        kernel,
        grid=(count // TILE,),
        in_specs=[pl.BlockSpec((TILE, width), lambda i: (i, 0)), fixed((width, 4 * hidden))],
        out_specs=[
            pl.BlockSpec((TILE, 2 * hidden), lambda i: (i, 0)),
            pl.BlockSpec((TILE, hidden), lambda i: (i, 0)),
            pl.BlockSpec((TILE, hidden), lambda i: (i, 0)),
        ],
        out_shape=[
            jax.ShapeDtypeStruct((count, 2 * hidden), BF),
            jax.ShapeDtypeStruct((count, hidden), BF),
            jax.ShapeDtypeStruct((count, hidden), BF),
        ],
        compiler_params=params(),
        cost_estimate=cost(8 * count * width * hidden, 2 * count * width + 12 * count * hidden),
        name="forward",
    )(rows, mats)


def part_rows(ad_own, ad_other, down_own, down_other):
    count, inner = ad_own.shape
    width = down_own.shape[1]

    def kernel(a_ref, b_ref, wa_ref, wb_ref, out_ref):
        out_ref[...] = (mm(a_ref[...], wa_ref[...]) + mm(b_ref[...], wb_ref[...])).astype(BF)

    return pl.pallas_call(
        kernel,
        grid=(count // TILE,),
        in_specs=[
            pl.BlockSpec((TILE, inner), lambda i: (i, 0)),
            pl.BlockSpec((TILE, inner), lambda i: (i, 0)),
            fixed((inner, width)),
            fixed((inner, width)),
        ],
        out_specs=pl.BlockSpec((TILE, width), lambda i: (i, 0)),
        out_shape=jax.ShapeDtypeStruct((count, width), BF),
        compiler_params=params(),
        cost_estimate=cost(4 * count * width * inner, 2 * count * width + 4 * inner * width),
        name="part_rows",
    )(ad_own, ad_other, down_own, down_other)


def gate_matrix(base, pos, gm, per):
    experts, toks = pos.shape
    step = TILE // per

    def kernel(base_ref, pos_ref, gm_ref, out_ref):
        match = slot_match(pos_ref[...], base_ref[0], per)
        weight = jnp.where(match, spread(gm_ref[...], per), 0.0).T
        high = weight.astype(BF)
        out_ref[:toks, :] = high
        out_ref[toks:, :] = (weight - high.astype(F32)).astype(BF)

    return pl.pallas_call(
        kernel,
        grid=(experts // step,),
        in_specs=[
            smem(),
            pl.BlockSpec((step, toks), lambda i: (i, 0)),
            pl.BlockSpec((step, toks), lambda i: (i, 0)),
        ],
        out_specs=pl.BlockSpec((2 * toks, TILE), lambda i: (0, i)),
        out_shape=jax.ShapeDtypeStruct((2 * toks, experts * per), BF),
        compiler_params=params(),
        cost_estimate=cost(4 * experts * per * toks, 4 * experts * per * toks),
        name="gate_matrix",
    )(base, pos, gm)


def combine(pairs):
    width = pairs[0][1].shape[1]
    toks = pairs[0][0].shape[0] // 2

    def kernel(*refs):
        both = None
        for n in range(0, len(refs) - 1, 2):
            term = mm(refs[n][...], refs[n + 1][...])
            both = term if both is None else both + term
        refs[-1][...] = both[:toks] + both[toks:]

    in_specs = []
    for matrix, rows in pairs:
        in_specs += [
            fixed(matrix.shape),
            pl.BlockSpec((rows.shape[0], COMBINE), lambda i: (0, i)),
        ]
    count = sum(rows.shape[0] for _, rows in pairs)
    return pl.pallas_call(
        kernel,
        grid=(width // COMBINE,),
        in_specs=in_specs,
        out_specs=pl.BlockSpec((toks, COMBINE), lambda i: (0, i)),
        out_shape=jax.ShapeDtypeStruct((toks, width), F32),
        compiler_params=params(),
        cost_estimate=cost(4 * count * toks * width, 2 * count * width),
        name="combine",
    )(*[array for pair in pairs for array in pair])


def weigh_pack(bases, pers, pos, gm, weight, own, other, half):
    experts, toks = pos.shape
    width = own.shape[1]
    chunks = len(pers)
    tile = WEIGH
    counts = [experts * per // tile for per in pers]
    firsts = [sum(counts[:n]) for n in range(chunks)]

    def kernel(*refs):
        base_refs = refs[:chunks]
        blocks = refs[chunks : 3 * chunks]
        tw_ref, own_ref, other_ref = refs[3 * chunks : 3 * chunks + 3]
        outs = refs[3 * chunks + 3 : -2]
        tangent_ref, split_ref = refs[-2:]
        i = pl.program_id(0)

        @pl.when(i == 0)
        def _():
            cols = pl.ds(pl.multiple_of(base_refs[0][1] * half, half), half)
            tangent_ref[...] = (own_ref[:, cols] + other_ref[:, cols]).astype(BF)
            scale = jnp.broadcast_to(tw_ref[...], (toks, toks)).T[:, :1]
            scaled = scale * (own_ref[...] + other_ref[...])
            high = scaled.astype(BF)
            split_ref[:toks, :] = high
            split_ref[toks:, :] = (scaled - high.astype(F32)).astype(BF)

        for n in range(chunks):

            @pl.when((i >= firsts[n]) & (i < firsts[n] + counts[n]))
            def _(n=n):
                match = slot_match(blocks[2 * n][...], base_refs[n][0], pers[n])
                hot = jnp.where(match, 1.0, 0.0).astype(BF)
                gates = spread(blocks[2 * n + 1][...], pers[n])
                gate = jnp.sum(jnp.where(match, gates, 0.0), axis=1, keepdims=True)
                row = mm(jnp.concatenate([hot, hot], axis=1), split_ref[...])
                outs[n][...] = (gate * row).astype(BF)

    def at(n):
        return lambda i: (jnp.clip(i - firsts[n], 0, counts[n] - 1), 0)

    pos_specs = []
    for n, per in enumerate(pers):
        pos_specs += [pl.BlockSpec((tile // per, toks), at(n))] * 2
    return pl.pallas_call(
        kernel,
        grid=(sum(counts),),
        in_specs=[smem() for _ in bases]
        + pos_specs
        + [fixed((1, toks)), fixed((toks, width)), fixed((toks, width))],
        out_specs=[pl.BlockSpec((tile, width), at(n)) for n in range(chunks)]
        + [pl.BlockSpec((toks, half), lambda i: (0, 0))],
        out_shape=[jax.ShapeDtypeStruct((experts * per, width), BF) for per in pers]
        + [jax.ShapeDtypeStruct((toks, half), BF)],
        scratch_shapes=[pltpu.VMEM((2 * toks, width), BF)],
        compiler_params=params(),
        cost_estimate=cost(4 * experts * sum(pers) * toks * width, 2 * experts * sum(pers) * width),
        name="weigh_pack",
    )(*bases, *[array for _ in pers for array in (pos, gm)], weight, own, other)


def gradients(q, silu, us, down):
    count, width = q.shape
    hidden = down.shape[0]
    tile = min(TILE, count)

    def kernel(q_ref, silu_ref, us_ref, down_ref, g_ref):
        back = mm_t(q_ref[...], down_ref[...])
        g_ref[:, :hidden] = (back * us_ref[...]).astype(BF)
        g_ref[:, hidden:] = (back * silu_ref[...]).astype(BF)

    return pl.pallas_call(
        kernel,
        grid=(count // tile,),
        in_specs=[
            pl.BlockSpec((tile, width), lambda i: (i, 0)),
            pl.BlockSpec((tile, hidden), lambda i: (i, 0)),
            pl.BlockSpec((tile, hidden), lambda i: (i, 0)),
            fixed((hidden, width)),
        ],
        out_specs=pl.BlockSpec((tile, 2 * hidden), lambda i: (i, 0)),
        out_shape=jax.ShapeDtypeStruct((count, 2 * hidden), BF),
        compiler_params=params(),
        cost_estimate=cost(2 * count * width * hidden, 2 * count * width),
        name="gradients",
    )(q, silu, us, down)


def phased_sums(own, other, down, factor):
    count, width = own[0].shape
    hidden = down.shape[0]
    tile = min(ROWS, count)
    piece = PIECE
    tiles = count // tile
    head = 2 * tiles

    def kernel(*refs):
        sides = (refs[:5], refs[5:10])
        down_ref = refs[10]
        outs = refs[11:14]
        g_ref, turned_ref, q_ref = refs[14:]
        i = pl.program_id(0)

        for side, (tile_ref, _, ad_ref, silu_ref, us_ref) in enumerate(sides):
            for n in range(tiles):

                @pl.when(i == side * tiles + n)
                def _(side=side, n=n, tile_ref=tile_ref, ad_ref=ad_ref, silu_ref=silu_ref, us_ref=us_ref):
                    rows = slice(side * count + n * tile, side * count + (n + 1) * tile)
                    q = tile_ref[...]
                    back = mm_t(q, down_ref[...])
                    g_ref[rows, :hidden] = (back * us_ref[...]).astype(BF)
                    g_ref[rows, hidden:] = (back * silu_ref[...]).astype(BF)
                    turned_ref[:, rows] = ad_ref[...].T
                    q_ref[rows, :] = q

        @pl.when(i >= head)
        def _():
            cols = pl.ds(pl.multiple_of(jnp.maximum(i - head, 0) * piece, piece), piece)
            gate_up = mm_rows(sides[0][1][...], g_ref[:count, :])
            gate_up += mm_rows(sides[1][1][...], g_ref[count:, :])
            outs[0][0] = factor * gate_up[:, :hidden]
            outs[1][0] = factor * gate_up[:, hidden:]
            outs[2][0] = factor * mm(turned_ref[...], q_ref[:, cols])

    def later(i):
        return jnp.maximum(i - head, 0)

    def specs(first):
        def at(i):
            return jnp.clip(i - first, 0, tiles - 1)

        return [
            pl.BlockSpec((tile, width), lambda i: (at(i), 0)),
            pl.BlockSpec((count, piece), lambda i: (0, later(i))),
            pl.BlockSpec((tile, hidden), lambda i: (at(i), 0)),
            pl.BlockSpec((tile, hidden), lambda i: (at(i), 0)),
            pl.BlockSpec((tile, hidden), lambda i: (at(i), 0)),
        ]

    shapes = [(1, width, hidden), (1, width, hidden), (1, hidden, width)]
    return pl.pallas_call(
        kernel,
        grid=(head + width // piece,),
        in_specs=specs(0) + specs(tiles) + [fixed((hidden, width))],
        out_specs=[
            pl.BlockSpec((1, piece, hidden), lambda i: (0, later(i), 0)),
            pl.BlockSpec((1, piece, hidden), lambda i: (0, later(i), 0)),
            pl.BlockSpec((1, hidden, piece), lambda i: (0, 0, later(i))),
        ],
        out_shape=[jax.ShapeDtypeStruct(shape, F32) for shape in shapes],
        scratch_shapes=[
            pltpu.VMEM((2 * count, 2 * hidden), BF),
            pltpu.VMEM((hidden, 2 * count), BF),
            pltpu.VMEM((2 * count, width), BF),
        ],
        compiler_params=params(),
        cost_estimate=cost(16 * count * width * hidden, 8 * count * width),
        name="phased_sums",
    )(*own, *other, down)


def last_sums(own, other, silu, us, down, start, factor):
    count, width = own[0].shape
    hidden = down.shape[0]
    piece = LAST_PIECE

    def kernel(*refs):
        q_ref, x_ref, g_ref, act_ref, q2_ref, x2_ref, act2_ref, silu_ref, us_ref, down_ref = refs[:10]
        begins, outs = refs[10:13], refs[13:16]
        g2_ref, turned_ref = refs[16:]
        i = pl.program_id(0)

        @pl.when(i == 0)
        def _():
            back = mm_t(q2_ref[...], down_ref[...])
            g2_ref[:, :hidden] = (back * us_ref[...]).astype(BF)
            g2_ref[:, hidden:] = (back * silu_ref[...]).astype(BF)
            turned_ref[:, :count] = act_ref[...].T
            turned_ref[:, count:] = act2_ref[...].T

        cols = pl.ds(pl.multiple_of(i * piece, piece), piece)
        gate_up = mm_rows(x_ref[...], g_ref[...]) + mm_rows(x2_ref[...], g2_ref[...])
        below = mm(turned_ref[:, :count], q_ref[...]) + mm(turned_ref[:, count:], q2_ref[:, cols])
        terms = (gate_up[:, :hidden], gate_up[:, hidden:], below)
        for out, term, begin in zip(outs, terms, begins):
            out[0] = factor * term + begin[0]

    column = pl.BlockSpec((count, piece), lambda i: (0, i))
    act = pl.BlockSpec((count, hidden), lambda i: (0, 0), pipeline_mode=pl.Buffered(buffer_count=1))
    results = [
        pl.BlockSpec((1, piece, hidden), lambda i: (0, i, 0)),
        pl.BlockSpec((1, piece, hidden), lambda i: (0, i, 0)),
        pl.BlockSpec((1, hidden, piece), lambda i: (0, 0, i)),
    ]
    shapes = [(1, width, hidden), (1, width, hidden), (1, hidden, width)]
    return pl.pallas_call(
        kernel,
        grid=(width // piece,),
        in_specs=[column, column, fixed((count, 2 * hidden)), act]
        + [fixed((count, width)), column, act]
        + [fixed((count, hidden)), fixed((count, hidden)), fixed((hidden, width))]
        + results,
        out_specs=results,
        out_shape=[jax.ShapeDtypeStruct(shape, F32) for shape in shapes],
        scratch_shapes=[
            pltpu.VMEM((count, 2 * hidden), BF),
            pltpu.VMEM((hidden, 2 * count), BF),
        ],
        compiler_params=params(),
        cost_estimate=cost(14 * count * width * hidden, 8 * count * width),
        name="last_sums",
    )(*own, *other, silu, us, down, *start)


def exchange(rows):
    return lax.all_to_all(rows, GROUP, split_axis=0, concat_axis=0, tiled=True)


def body(tokens, expert_ids, gates, token_weight, w_gate, w_up, w_down, v_gate, v_up, v_down):
    toks, width = tokens.shape
    picks = expert_ids.shape[1]
    experts = lax.axis_size("dp") * lax.axis_size("expert")
    cores = lax.axis_size("tensor")
    hidden = w_gate.shape[2]
    per_core = min(3 * toks * picks // experts, toks) // cores
    core = lax.axis_index("tensor")
    factor = 1.0 / (toks * picks) ** 0.5

    def swap(rows):
        return lax.ppermute(rows, "tensor", [(0, 1), (1, 0)])

    chunks = []
    start = 0
    for per in SLOTS:
        size = per * per_core // sum(SLOTS)
        chunks.append((jnp.stack([core * per_core + start, core]).astype(jnp.int32), size))
        start += size

    base, per = chunks[0]
    packed, pos, gm = route_pack(base, expert_ids.T, gates.T, tokens, experts, per)
    arrived = exchange(packed)
    later = [pack(base, pos, tokens, per) for base, per in chunks[1:]]
    mats = jnp.concatenate([w_gate[0], w_up[0], v_gate[0], v_up[0]], axis=1)
    down_own = jnp.concatenate([v_down[0], w_down[0]], axis=0)
    matrices = [gate_matrix(base, pos, gm, per) for base, per in chunks]
    arrived, later, mats, down_own, matrices = lax.optimization_barrier(
        (arrived, later, mats, down_own, matrices)
    )
    weight = token_weight[None, :]
    down_other = swap(down_own)

    def run_forward(x_own):
        x_other = swap(x_own)
        mine = forward(x_own, mats, hidden)
        theirs = forward(x_other, mats, hidden)
        part = part_rows(mine[0], swap(theirs[0]), down_own, down_other)
        return part, (x_own, *mine), (x_other, *theirs)

    sides = []
    x_large = exchange(later[0])
    part, mine, theirs = run_forward(arrived)
    sides.append((mine, theirs))
    x_large, part = lax.optimization_barrier((x_large, part))
    returned = exchange(part)
    part, mine, theirs = run_forward(x_large)
    sides.append((mine, theirs))
    returned, part = lax.optimization_barrier((returned, part))
    last = exchange(part)
    last, returned = lax.optimization_barrier((last, returned))
    own = combine(list(zip(matrices, (returned, last))))
    other = swap(own)

    order = (1, 0)
    bases, pers = zip(*[chunks[n] for n in order])
    send_large, send_small, tangent = weigh_pack(
        bases, pers, pos, gm, weight, own, other, width // cores
    )
    q_large = exchange(send_large)
    q_large, send_small = lax.optimization_barrier((q_large, send_small))
    q_small = exchange(send_small)
    down = w_down[0]
    mine, theirs = sides[1]
    sums = phased_sums((q_large, *mine), (swap(q_large), *theirs), down, factor)
    q_small, sums = lax.optimization_barrier((q_small, sums))
    q_other = swap(q_small)
    x, ad, silu, us = sides[0][0]
    own_side = (q_small, x, gradients(q_small, silu, us, down), ad)
    x, ad, silu, us = sides[0][1]
    gv_gate, gv_up, gv_down = last_sums(
        own_side, (q_other, x, ad), silu, us, down, sums, factor
    )
    return gv_gate, gv_up, gv_down, tangent


def solution(mesh):
    rows = P(GROUP, None)
    cols = P(GROUP, None, "tensor")
    down = P(GROUP, "tensor", None)
    in_specs = (rows, rows, rows, P(GROUP), cols, cols, down, cols, cols, down)
    out_specs = (cols, cols, down, P(GROUP, "tensor"))
    return jax.shard_map(body, mesh=mesh, in_specs=in_specs, out_specs=out_specs, check_vma=False)
```

```python
import jax
import jax.numpy as jnp
from jax import lax
from jax.experimental import pallas as pl
from jax.experimental.pallas import tpu as pltpu
from jax.sharding import PartitionSpec as P

BF = jnp.bfloat16
F32 = jnp.float32
GROUP = ("dp", "expert")
VMEM_LIMIT = 63 * 1024 * 1024
TILE = 256
PIECE = 512
LAST_PIECE = 1024
ROWS = 512
SLOTS = (1, 2)
COMBINE = 1024
WEIGH = 512


def params():
    return pltpu.CompilerParams(
        dimension_semantics=("arbitrary",), vmem_limit_bytes=VMEM_LIMIT
    )


def cost(flops, nbytes):
    return pl.CostEstimate(flops=flops // 16, bytes_accessed=nbytes // 16, transcendentals=0)


def fixed(shape):
    return pl.BlockSpec(
        shape, lambda i: (0,) * len(shape), pipeline_mode=pl.Buffered(buffer_count=1)
    )


def smem():
    return pl.BlockSpec(memory_space=pltpu.SMEM)


def mm(left, right):
    return jnp.dot(left, right, preferred_element_type=F32)


def mm_t(left, right):
    return lax.dot_general(left, right, (((1,), (1,)), ((), ())), preferred_element_type=F32)


def mm_rows(left, right):
    return lax.dot_general(left, right, (((0,), (0,)), ((), ())), preferred_element_type=F32)


def spread(rows, per):
    count, toks = rows.shape
    return jnp.broadcast_to(rows[:, None, :], (count, per, toks)).reshape(count * per, toks)


def slot_match(pos, base, per):
    count, toks = pos.shape
    slot = lax.broadcasted_iota(jnp.int32, (count, per, toks), 1).reshape(count * per, toks)
    return spread(pos, per) == (slot + base).astype(F32)


def route_pack(base, ids_t, gates_t, tokens, experts, per):
    picks, toks = ids_t.shape
    width = tokens.shape[1]
    step = TILE // per
    steps = experts // step

    def kernel(base_ref, ids_ref, gates_ref, tok_ref, x_ref, pos_ref, gm_ref):
        i = pl.program_id(0)

        @pl.when(i == 0)
        def _():
            label = lax.broadcasted_iota(jnp.int32, (experts, toks), 0)
            hits = jnp.zeros((experts, toks), F32)
            gm = jnp.zeros((experts, toks), F32)
            for k in range(picks):
                match = ids_ref[k : k + 1, :] == label
                hits = jnp.where(match, 1.0, hits)
                gm = jnp.where(match, gates_ref[k : k + 1, :], gm)
            row = lax.broadcasted_iota(jnp.int32, (toks, toks), 0)
            col = lax.broadcasted_iota(jnp.int32, (toks, toks), 1)
            before = jnp.where(row < col, 1.0, 0.0).astype(BF)
            pos = mm(hits.astype(BF), before)
            pos_ref[...] = jnp.where(hits > 0.5, pos, -1.0)
            gm_ref[...] = gm

        pos = pos_ref[pl.ds(pl.multiple_of(i * step, step), step), :]
        hot = jnp.where(slot_match(pos, base_ref[0], per), 1.0, 0.0).astype(BF)
        x_ref[...] = mm(hot, tok_ref[...]).astype(BF)

    return pl.pallas_call(
        kernel,
        grid=(steps,),
        in_specs=[smem(), fixed((picks, toks)), fixed((picks, toks)), fixed((toks, width))],
        out_specs=[
            pl.BlockSpec((TILE, width), lambda i: (i, 0)),
            pl.BlockSpec((experts, toks), lambda i: (0, 0)),
            pl.BlockSpec((experts, toks), lambda i: (0, 0)),
        ],
        out_shape=[
            jax.ShapeDtypeStruct((experts * per, width), BF),
            jax.ShapeDtypeStruct((experts, toks), F32),
            jax.ShapeDtypeStruct((experts, toks), F32),
        ],
        compiler_params=params(),
        cost_estimate=cost(2 * experts * per * toks * width, 2 * experts * per * width),
        name="route_pack",
    )(base, ids_t, gates_t, tokens)


def pack(base, pos, tokens, per):
    experts, toks = pos.shape
    width = tokens.shape[1]
    step = TILE // per

    def kernel(base_ref, pos_ref, tok_ref, x_ref):
        hot = jnp.where(slot_match(pos_ref[...], base_ref[0], per), 1.0, 0.0).astype(BF)
        x_ref[...] = mm(hot, tok_ref[...]).astype(BF)

    return pl.pallas_call(
        kernel,
        grid=(experts // step,),
        in_specs=[smem(), pl.BlockSpec((step, toks), lambda i: (i, 0)), fixed((toks, width))],
        out_specs=pl.BlockSpec((TILE, width), lambda i: (i, 0)),
        out_shape=jax.ShapeDtypeStruct((experts * per, width), BF),
        compiler_params=params(),
        cost_estimate=cost(2 * experts * per * toks * width, 2 * experts * per * width),
        name="pack",
    )(base, pos, tokens)


def forward(rows, mats_own, mats_other, down_own, down_other):
    count, width = rows.shape
    hidden = mats_own.shape[1] // 4

    def kernel(x_ref, *refs):
        sources = refs[:4]
        part_ref, own_ref, other_ref = refs[4:7]
        held, sems = refs[7:11], refs[11]
        first = pl.program_id(0) == 0
        copies = [
            pltpu.make_async_copy(source, target, sems.at[n])
            for n, (source, target) in enumerate(zip(sources, held))
        ]

        @pl.when(first)
        def _():
            for copy in copies:
                copy.start()

        def ready(n):
            @pl.when(first)
            def _():
                copies[n].wait()

        def side(n, aux_ref):
            ready(n)
            pre = mm(x_ref[...], held[n][...])
            gate = pre[:, :hidden]
            up = pre[:, hidden : 2 * hidden]
            d_gate = pre[:, 2 * hidden : 3 * hidden]
            d_up = pre[:, 3 * hidden :]
            sigma = jax.nn.sigmoid(gate)
            silu = gate * sigma
            us = sigma * (1.0 + gate * (1.0 - sigma)) * up
            act = (silu * up).astype(BF)
            aux_ref[:, :hidden] = act
            aux_ref[:, hidden : 2 * hidden] = silu.astype(BF)
            aux_ref[:, 2 * hidden :] = us.astype(BF)
            d_act = (us * d_gate + silu * d_up).astype(BF)
            return jnp.concatenate([act, d_act], axis=1)

        left = side(0, own_ref)
        right = side(1, other_ref)
        ready(2)
        ready(3)
        part_ref[...] = (mm(left, held[2][...]) + mm(right, held[3][...])).astype(BF)

    weights = [mats_own, mats_other, down_own, down_other]
    return pl.pallas_call(
        kernel,
        grid=(count // TILE,),
        in_specs=[pl.BlockSpec((TILE, width), lambda i: (i, 0))]
        + [pl.BlockSpec(memory_space=pl.ANY) for _ in weights],
        out_specs=[
            pl.BlockSpec((TILE, width), lambda i: (i, 0)),
            pl.BlockSpec((TILE, 3 * hidden), lambda i: (i, 0)),
            pl.BlockSpec((TILE, 3 * hidden), lambda i: (i, 0)),
        ],
        out_shape=[
            jax.ShapeDtypeStruct((count, width), BF),
            jax.ShapeDtypeStruct((count, 3 * hidden), BF),
            jax.ShapeDtypeStruct((count, 3 * hidden), BF),
        ],
        scratch_shapes=[pltpu.VMEM(w.shape, BF) for w in weights]
        + [pltpu.SemaphoreType.DMA((len(weights),))],
        compiler_params=params(),
        cost_estimate=cost(24 * count * width * hidden, 8 * count * width),
        name="forward",
    )(rows, *weights)


def gate_matrix(base, pos, gm, per):
    experts, toks = pos.shape
    step = TILE // per

    def kernel(base_ref, pos_ref, gm_ref, out_ref):
        match = slot_match(pos_ref[...], base_ref[0], per)
        weight = jnp.where(match, spread(gm_ref[...], per), 0.0).T
        high = weight.astype(BF)
        out_ref[:toks, :] = high
        out_ref[toks:, :] = (weight - high.astype(F32)).astype(BF)

    return pl.pallas_call(
        kernel,
        grid=(experts // step,),
        in_specs=[
            smem(),
            pl.BlockSpec((step, toks), lambda i: (i, 0)),
            pl.BlockSpec((step, toks), lambda i: (i, 0)),
        ],
        out_specs=pl.BlockSpec((2 * toks, TILE), lambda i: (0, i)),
        out_shape=jax.ShapeDtypeStruct((2 * toks, experts * per), BF),
        compiler_params=params(),
        cost_estimate=cost(4 * experts * per * toks, 4 * experts * per * toks),
        name="gate_matrix",
    )(base, pos, gm)


def combine(pairs):
    width = pairs[0][1].shape[1]
    toks = pairs[0][0].shape[0] // 2

    def kernel(*refs):
        both = None
        for n in range(0, len(refs) - 1, 2):
            term = mm(refs[n][...], refs[n + 1][...])
            both = term if both is None else both + term
        refs[-1][...] = both[:toks] + both[toks:]

    in_specs = []
    for matrix, rows in pairs:
        in_specs += [
            fixed(matrix.shape),
            pl.BlockSpec((rows.shape[0], COMBINE), lambda i: (0, i)),
        ]
    count = sum(rows.shape[0] for _, rows in pairs)
    return pl.pallas_call(
        kernel,
        grid=(width // COMBINE,),
        in_specs=in_specs,
        out_specs=pl.BlockSpec((toks, COMBINE), lambda i: (0, i)),
        out_shape=jax.ShapeDtypeStruct((toks, width), F32),
        compiler_params=params(),
        cost_estimate=cost(4 * count * toks * width, 2 * count * width),
        name="combine",
    )(*[array for pair in pairs for array in pair])


def weigh_pack(bases, pers, pos, gm, weight, own, other, half):
    experts, toks = pos.shape
    width = own.shape[1]
    chunks = len(pers)
    tile = WEIGH
    counts = [experts * per // tile for per in pers]
    firsts = [sum(counts[:n]) for n in range(chunks)]

    def kernel(*refs):
        base_refs = refs[:chunks]
        blocks = refs[chunks : 3 * chunks]
        tw_ref, own_ref, other_ref = refs[3 * chunks : 3 * chunks + 3]
        outs = refs[3 * chunks + 3 : -2]
        tangent_ref, split_ref = refs[-2:]
        i = pl.program_id(0)

        @pl.when(i == 0)
        def _():
            cols = pl.ds(pl.multiple_of(base_refs[0][1] * half, half), half)
            tangent_ref[...] = (own_ref[:, cols] + other_ref[:, cols]).astype(BF)
            scale = jnp.broadcast_to(tw_ref[...], (toks, toks)).T[:, :1]
            scaled = scale * (own_ref[...] + other_ref[...])
            high = scaled.astype(BF)
            split_ref[:toks, :] = high
            split_ref[toks:, :] = (scaled - high.astype(F32)).astype(BF)

        for n in range(chunks):

            @pl.when((i >= firsts[n]) & (i < firsts[n] + counts[n]))
            def _(n=n):
                match = slot_match(blocks[2 * n][...], base_refs[n][0], pers[n])
                hot = jnp.where(match, 1.0, 0.0).astype(BF)
                gates = spread(blocks[2 * n + 1][...], pers[n])
                gate = jnp.sum(jnp.where(match, gates, 0.0), axis=1, keepdims=True)
                row = mm(jnp.concatenate([hot, hot], axis=1), split_ref[...])
                outs[n][...] = (gate * row).astype(BF)

    def at(n):
        return lambda i: (jnp.clip(i - firsts[n], 0, counts[n] - 1), 0)

    pos_specs = []
    for n, per in enumerate(pers):
        pos_specs += [pl.BlockSpec((tile // per, toks), at(n))] * 2
    return pl.pallas_call(
        kernel,
        grid=(sum(counts),),
        in_specs=[smem() for _ in bases]
        + pos_specs
        + [fixed((1, toks)), fixed((toks, width)), fixed((toks, width))],
        out_specs=[pl.BlockSpec((tile, width), at(n)) for n in range(chunks)]
        + [pl.BlockSpec((toks, half), lambda i: (0, 0))],
        out_shape=[jax.ShapeDtypeStruct((experts * per, width), BF) for per in pers]
        + [jax.ShapeDtypeStruct((toks, half), BF)],
        scratch_shapes=[pltpu.VMEM((2 * toks, width), BF)],
        compiler_params=params(),
        cost_estimate=cost(4 * experts * sum(pers) * toks * width, 2 * experts * sum(pers) * width),
        name="weigh_pack",
    )(*bases, *[array for _ in pers for array in (pos, gm)], weight, own, other)


def gradients(q, aux, down):
    count, width = q.shape
    hidden = down.shape[0]
    tile = min(TILE, count)

    def kernel(q_ref, silu_ref, us_ref, down_ref, g_ref):
        back = mm_t(q_ref[...], down_ref[...])
        g_ref[:, :hidden] = (back * us_ref[...]).astype(BF)
        g_ref[:, hidden:] = (back * silu_ref[...]).astype(BF)

    return pl.pallas_call(
        kernel,
        grid=(count // tile,),
        in_specs=[
            pl.BlockSpec((tile, width), lambda i: (i, 0)),
            pl.BlockSpec((tile, hidden), lambda i: (i, 1)),
            pl.BlockSpec((tile, hidden), lambda i: (i, 2)),
            fixed((hidden, width)),
        ],
        out_specs=pl.BlockSpec((tile, 2 * hidden), lambda i: (i, 0)),
        out_shape=jax.ShapeDtypeStruct((count, 2 * hidden), BF),
        compiler_params=params(),
        cost_estimate=cost(2 * count * width * hidden, 2 * count * width),
        name="gradients",
    )(q, aux, aux, down)


def phased_sums(own, other, down, factor):
    count, width = own[0].shape
    hidden = down.shape[0]
    tile = min(ROWS, count)
    piece = PIECE
    tiles = count // tile
    head = 2 * tiles

    def kernel(*refs):
        sides = (refs[:5], refs[5:10])
        down_ref = refs[10]
        outs = refs[11:14]
        g_ref, turned_ref, q_ref = refs[14:]
        i = pl.program_id(0)

        for side, (tile_ref, _, ad_ref, silu_ref, us_ref) in enumerate(sides):
            for n in range(tiles):

                @pl.when(i == side * tiles + n)
                def _(side=side, n=n, tile_ref=tile_ref, ad_ref=ad_ref, silu_ref=silu_ref, us_ref=us_ref):
                    rows = slice(side * count + n * tile, side * count + (n + 1) * tile)
                    q = tile_ref[...]
                    back = mm_t(q, down_ref[...])
                    g_ref[rows, :hidden] = (back * us_ref[...]).astype(BF)
                    g_ref[rows, hidden:] = (back * silu_ref[...]).astype(BF)
                    turned_ref[:, rows] = ad_ref[...].T
                    q_ref[rows, :] = q

        @pl.when(i >= head)
        def _():
            cols = pl.ds(pl.multiple_of(jnp.maximum(i - head, 0) * piece, piece), piece)
            gate_up = mm_rows(sides[0][1][...], g_ref[:count, :])
            gate_up += mm_rows(sides[1][1][...], g_ref[count:, :])
            outs[0][0] = factor * gate_up[:, :hidden]
            outs[1][0] = factor * gate_up[:, hidden:]
            outs[2][0] = factor * mm(turned_ref[...], q_ref[:, cols])

    def later(i):
        return jnp.maximum(i - head, 0)

    def specs(first):
        def at(i):
            return jnp.clip(i - first, 0, tiles - 1)

        return [
            pl.BlockSpec((tile, width), lambda i: (at(i), 0)),
            pl.BlockSpec((count, piece), lambda i: (0, later(i))),
            pl.BlockSpec((tile, hidden), lambda i: (at(i), 0)),
            pl.BlockSpec((tile, hidden), lambda i: (at(i), 1)),
            pl.BlockSpec((tile, hidden), lambda i: (at(i), 2)),
        ]

    shapes = [(1, width, hidden), (1, width, hidden), (1, hidden, width)]
    return pl.pallas_call(
        kernel,
        grid=(head + width // piece,),
        in_specs=specs(0) + specs(tiles) + [fixed((hidden, width))],
        out_specs=[
            pl.BlockSpec((1, piece, hidden), lambda i: (0, later(i), 0)),
            pl.BlockSpec((1, piece, hidden), lambda i: (0, later(i), 0)),
            pl.BlockSpec((1, hidden, piece), lambda i: (0, 0, later(i))),
        ],
        out_shape=[jax.ShapeDtypeStruct(shape, F32) for shape in shapes],
        scratch_shapes=[
            pltpu.VMEM((2 * count, 2 * hidden), BF),
            pltpu.VMEM((hidden, 2 * count), BF),
            pltpu.VMEM((2 * count, width), BF),
        ],
        compiler_params=params(),
        cost_estimate=cost(16 * count * width * hidden, 8 * count * width),
        name="phased_sums",
    )(*own, own[2], own[2], *other, other[2], other[2], down)


def last_sums(own, other, down, start, factor):
    count, width = own[0].shape
    hidden = down.shape[0]
    piece = LAST_PIECE

    def kernel(*refs):
        q_ref, x_ref, g_ref, act_ref, q2_ref, x2_ref, act2_ref, silu_ref, us_ref, down_ref = refs[:10]
        begins, outs = refs[10:13], refs[13:16]
        g2_ref, turned_ref = refs[16:]
        i = pl.program_id(0)

        @pl.when(i == 0)
        def _():
            back = mm_t(q2_ref[...], down_ref[...])
            g2_ref[:, :hidden] = (back * us_ref[...]).astype(BF)
            g2_ref[:, hidden:] = (back * silu_ref[...]).astype(BF)
            turned_ref[:, :count] = act_ref[...].T
            turned_ref[:, count:] = act2_ref[...].T

        cols = pl.ds(pl.multiple_of(i * piece, piece), piece)
        gate_up = mm_rows(x_ref[...], g_ref[...]) + mm_rows(x2_ref[...], g2_ref[...])
        below = mm(turned_ref[:, :count], q_ref[...]) + mm(turned_ref[:, count:], q2_ref[:, cols])
        terms = (gate_up[:, :hidden], gate_up[:, hidden:], below)
        for out, term, begin in zip(outs, terms, begins):
            out[0] = factor * term + begin[0]

    column = pl.BlockSpec((count, piece), lambda i: (0, i))

    def third(n):
        once = pl.Buffered(buffer_count=1)
        return pl.BlockSpec((count, hidden), lambda i: (0, n), pipeline_mode=once)

    results = [
        pl.BlockSpec((1, piece, hidden), lambda i: (0, i, 0)),
        pl.BlockSpec((1, piece, hidden), lambda i: (0, i, 0)),
        pl.BlockSpec((1, hidden, piece), lambda i: (0, 0, i)),
    ]
    shapes = [(1, width, hidden), (1, width, hidden), (1, hidden, width)]
    return pl.pallas_call(
        kernel,
        grid=(width // piece,),
        in_specs=[column, column, fixed((count, 2 * hidden)), third(0)]
        + [fixed((count, width)), column, third(0)]
        + [third(1), third(2), fixed((hidden, width))]
        + results,
        out_specs=results,
        out_shape=[jax.ShapeDtypeStruct(shape, F32) for shape in shapes],
        scratch_shapes=[
            pltpu.VMEM((count, 2 * hidden), BF),
            pltpu.VMEM((hidden, 2 * count), BF),
        ],
        compiler_params=params(),
        cost_estimate=cost(14 * count * width * hidden, 8 * count * width),
        name="last_sums",
    )(*own, *other, other[2], other[2], down, *start)


def exchange(rows):
    return lax.all_to_all(rows, GROUP, split_axis=0, concat_axis=0, tiled=True)


def body(tokens, expert_ids, gates, token_weight, w_gate, w_up, w_down, v_gate, v_up, v_down):
    toks, width = tokens.shape
    picks = expert_ids.shape[1]
    experts = lax.axis_size("dp") * lax.axis_size("expert")
    cores = lax.axis_size("tensor")
    hidden = w_gate.shape[2]
    per_core = min(3 * toks * picks // experts, toks) // cores
    core = lax.axis_index("tensor")
    factor = 1.0 / (toks * picks) ** 0.5

    def swap(rows):
        return lax.ppermute(rows, "tensor", [(0, 1), (1, 0)])

    chunks = []
    start = 0
    for per in SLOTS:
        size = per * per_core // sum(SLOTS)
        chunks.append((jnp.stack([core * per_core + start, core]).astype(jnp.int32), size))
        start += size

    base, per = chunks[0]
    packed, pos, gm = route_pack(base, expert_ids.T, gates.T, tokens, experts, per)
    arrived = exchange(packed)
    later = [pack(base, pos, tokens, per) for base, per in chunks[1:]]
    mats = jnp.concatenate([w_gate[0], w_up[0], v_gate[0], v_up[0]], axis=1)
    downs = jnp.concatenate([v_down[0], w_down[0]], axis=0)
    matrices = [gate_matrix(base, pos, gm, per) for base, per in chunks]
    arrived, later, mats, downs, matrices = lax.optimization_barrier(
        (arrived, later, mats, downs, matrices)
    )
    weight = token_weight[None, :]
    x_large = exchange(later[0])
    mats_other, downs_other = swap(mats), swap(downs)

    x_small = arrived
    part, aux_small, sent = forward(x_small, mats, mats_other, downs, downs_other)
    theirs_small = swap(x_small), swap(sent)
    x_large, part, theirs_small = lax.optimization_barrier((x_large, part, theirs_small))
    returned = exchange(part)
    x_their = swap(x_large)
    part, aux_large, sent = forward(x_large, mats, mats_other, downs, downs_other)
    returned, part, x_their = lax.optimization_barrier((returned, part, x_their))
    last = exchange(part)
    last, returned = lax.optimization_barrier((last, returned))
    own = combine(list(zip(matrices, (returned, last))))
    other = swap(own)

    order = (1, 0)
    bases, pers = zip(*[chunks[n] for n in order])
    send_large, send_small, tangent = weigh_pack(
        bases, pers, pos, gm, weight, own, other, width // cores
    )
    q_large = exchange(send_large)
    q_large, send_small, sent = lax.optimization_barrier((q_large, send_small, sent))
    q_small = exchange(send_small)
    down = w_down[0]
    sums = phased_sums(
        (q_large, x_large, aux_large), (swap(q_large), x_their, swap(sent)), down, factor
    )
    q_small, sums = lax.optimization_barrier((q_small, sums))
    q_other = swap(q_small)
    own_side = (q_small, x_small, gradients(q_small, aux_small, down), aux_small)
    gv_gate, gv_up, gv_down = last_sums(own_side, (q_other, *theirs_small), down, sums, factor)
    return gv_gate, gv_up, gv_down, tangent


def solution(mesh):
    rows = P(GROUP, None)
    cols = P(GROUP, None, "tensor")
    down = P(GROUP, "tensor", None)
    in_specs = (rows, rows, rows, P(GROUP), cols, cols, down, cols, cols, down)
    out_specs = (cols, cols, down, P(GROUP, "tensor"))
    return jax.shard_map(body, mesh=mesh, in_specs=in_specs, out_specs=out_specs, check_vma=False)
```

```python
import jax
import jax.numpy as jnp
from jax import lax
from jax.experimental import pallas as pl
from jax.experimental.pallas import tpu as pltpu
from jax.sharding import PartitionSpec as P

BF = jnp.bfloat16
F32 = jnp.float32
GROUP = ("dp", "expert")
VMEM_LIMIT = 63 * 1024 * 1024
TILE = 512
PIECE = 512
LAST_PIECE = 512
ROWS = 512
SLOTS = (1, 2)
COMBINE = 1024
WEIGH = 512


def params():
    return pltpu.CompilerParams(
        dimension_semantics=("arbitrary",), vmem_limit_bytes=VMEM_LIMIT
    )


def cost(flops, nbytes):
    return pl.CostEstimate(flops=flops // 16, bytes_accessed=nbytes // 16, transcendentals=0)


def fixed(shape):
    return pl.BlockSpec(
        shape, lambda i: (0,) * len(shape), pipeline_mode=pl.Buffered(buffer_count=1)
    )


def smem():
    return pl.BlockSpec(memory_space=pltpu.SMEM)


def mm(left, right):
    return jnp.dot(left, right, preferred_element_type=F32)


def mm_t(left, right):
    return lax.dot_general(left, right, (((1,), (1,)), ((), ())), preferred_element_type=F32)


def mm_rows(left, right):
    return lax.dot_general(left, right, (((0,), (0,)), ((), ())), preferred_element_type=F32)


def spread(rows, per):
    count, toks = rows.shape
    return jnp.broadcast_to(rows[:, None, :], (count, per, toks)).reshape(count * per, toks)


def slot_match(pos, base, per):
    count, toks = pos.shape
    slot = lax.broadcasted_iota(jnp.int32, (count, per, toks), 1).reshape(count * per, toks)
    return spread(pos, per) == (slot + base).astype(F32)


def route_pack(base, ids_t, gates_t, tokens, experts, per):
    picks, toks = ids_t.shape
    width = tokens.shape[1]
    step = TILE // per
    steps = experts // step

    def kernel(base_ref, ids_ref, gates_ref, tok_ref, x_ref, pos_ref, gm_ref):
        i = pl.program_id(0)

        @pl.when(i == 0)
        def _():
            label = lax.broadcasted_iota(jnp.int32, (experts, toks), 0)
            hits = jnp.zeros((experts, toks), F32)
            gm = jnp.zeros((experts, toks), F32)
            for k in range(picks):
                match = ids_ref[k : k + 1, :] == label
                hits = jnp.where(match, 1.0, hits)
                gm = jnp.where(match, gates_ref[k : k + 1, :], gm)
            row = lax.broadcasted_iota(jnp.int32, (toks, toks), 0)
            col = lax.broadcasted_iota(jnp.int32, (toks, toks), 1)
            before = jnp.where(row < col, 1.0, 0.0).astype(BF)
            pos = mm(hits.astype(BF), before)
            pos_ref[...] = jnp.where(hits > 0.5, pos, -1.0)
            gm_ref[...] = gm

        pos = pos_ref[pl.ds(pl.multiple_of(i * step, step), step), :]
        hot = jnp.where(slot_match(pos, base_ref[0], per), 1.0, 0.0).astype(BF)
        x_ref[...] = mm(hot, tok_ref[...]).astype(BF)

    return pl.pallas_call(
        kernel,
        grid=(steps,),
        in_specs=[smem(), fixed((picks, toks)), fixed((picks, toks)), fixed((toks, width))],
        out_specs=[
            pl.BlockSpec((TILE, width), lambda i: (i, 0)),
            pl.BlockSpec((experts, toks), lambda i: (0, 0)),
            pl.BlockSpec((experts, toks), lambda i: (0, 0)),
        ],
        out_shape=[
            jax.ShapeDtypeStruct((experts * per, width), BF),
            jax.ShapeDtypeStruct((experts, toks), F32),
            jax.ShapeDtypeStruct((experts, toks), F32),
        ],
        compiler_params=params(),
        cost_estimate=cost(2 * experts * per * toks * width, 2 * experts * per * width),
        name="route_pack",
    )(base, ids_t, gates_t, tokens)


def pack(base, pos, tokens, per):
    experts, toks = pos.shape
    width = tokens.shape[1]
    step = TILE // per

    def kernel(base_ref, pos_ref, tok_ref, x_ref):
        hot = jnp.where(slot_match(pos_ref[...], base_ref[0], per), 1.0, 0.0).astype(BF)
        x_ref[...] = mm(hot, tok_ref[...]).astype(BF)

    return pl.pallas_call(
        kernel,
        grid=(experts // step,),
        in_specs=[smem(), pl.BlockSpec((step, toks), lambda i: (i, 0)), fixed((toks, width))],
        out_specs=pl.BlockSpec((TILE, width), lambda i: (i, 0)),
        out_shape=jax.ShapeDtypeStruct((experts * per, width), BF),
        compiler_params=params(),
        cost_estimate=cost(2 * experts * per * toks * width, 2 * experts * per * width),
        name="pack",
    )(base, pos, tokens)


def forward(rows, mats_own, mats_other, down_own, down_other):
    count, width = rows.shape
    hidden = mats_own.shape[1] // 4

    def kernel(x_ref, *refs):
        sources = refs[:4]
        part_ref, own_ref, other_ref = refs[4:7]
        held, sems = refs[7:11], refs[11]
        first = pl.program_id(0) == 0
        copies = [
            pltpu.make_async_copy(source, target, sems.at[n])
            for n, (source, target) in enumerate(zip(sources, held))
        ]

        @pl.when(first)
        def _():
            for copy in copies:
                copy.start()

        def ready(n):
            @pl.when(first)
            def _():
                copies[n].wait()

        def side(n, aux_ref):
            ready(n)
            pre = mm(x_ref[...], held[n][...])
            gate = pre[:, :hidden]
            up = pre[:, hidden : 2 * hidden]
            d_gate = pre[:, 2 * hidden : 3 * hidden]
            d_up = pre[:, 3 * hidden :]
            sigma = jax.nn.sigmoid(gate)
            silu = gate * sigma
            us = sigma * (1.0 + gate * (1.0 - sigma)) * up
            act = (silu * up).astype(BF)
            aux_ref[:, :hidden] = act
            aux_ref[:, hidden : 2 * hidden] = silu.astype(BF)
            aux_ref[:, 2 * hidden :] = us.astype(BF)
            d_act = (us * d_gate + silu * d_up).astype(BF)
            return jnp.concatenate([act, d_act], axis=1)

        left = side(0, own_ref)
        right = side(1, other_ref)
        ready(2)
        ready(3)
        part_ref[...] = (mm(left, held[2][...]) + mm(right, held[3][...])).astype(BF)

    weights = [mats_own, mats_other, down_own, down_other]
    return pl.pallas_call(
        kernel,
        grid=(count // TILE,),
        in_specs=[pl.BlockSpec((TILE, width), lambda i: (i, 0))]
        + [pl.BlockSpec(memory_space=pl.ANY) for _ in weights],
        out_specs=[
            pl.BlockSpec((TILE, width), lambda i: (i, 0)),
            pl.BlockSpec((TILE, 3 * hidden), lambda i: (i, 0)),
            pl.BlockSpec((TILE, 3 * hidden), lambda i: (i, 0)),
        ],
        out_shape=[
            jax.ShapeDtypeStruct((count, width), BF),
            jax.ShapeDtypeStruct((count, 3 * hidden), BF),
            jax.ShapeDtypeStruct((count, 3 * hidden), BF),
        ],
        scratch_shapes=[pltpu.VMEM(w.shape, BF) for w in weights]
        + [pltpu.SemaphoreType.DMA((len(weights),))],
        compiler_params=params(),
        cost_estimate=cost(24 * count * width * hidden, 8 * count * width),
        name="forward",
    )(rows, *weights)


def gate_matrix(base, pos, gm, per):
    experts, toks = pos.shape
    step = TILE // per

    def kernel(base_ref, pos_ref, gm_ref, out_ref):
        match = slot_match(pos_ref[...], base_ref[0], per)
        weight = jnp.where(match, spread(gm_ref[...], per), 0.0).T
        high = weight.astype(BF)
        out_ref[:toks, :] = high
        out_ref[toks:, :] = (weight - high.astype(F32)).astype(BF)

    return pl.pallas_call(
        kernel,
        grid=(experts // step,),
        in_specs=[
            smem(),
            pl.BlockSpec((step, toks), lambda i: (i, 0)),
            pl.BlockSpec((step, toks), lambda i: (i, 0)),
        ],
        out_specs=pl.BlockSpec((2 * toks, TILE), lambda i: (0, i)),
        out_shape=jax.ShapeDtypeStruct((2 * toks, experts * per), BF),
        compiler_params=params(),
        cost_estimate=cost(4 * experts * per * toks, 4 * experts * per * toks),
        name="gate_matrix",
    )(base, pos, gm)


def combine(pairs):
    width = pairs[0][1].shape[1]
    toks = pairs[0][0].shape[0] // 2

    def kernel(*refs):
        both = None
        for n in range(0, len(refs) - 1, 2):
            term = mm(refs[n][...], refs[n + 1][...])
            both = term if both is None else both + term
        refs[-1][...] = both[:toks] + both[toks:]

    in_specs = []
    for matrix, rows in pairs:
        in_specs += [
            fixed(matrix.shape),
            pl.BlockSpec((rows.shape[0], COMBINE), lambda i: (0, i)),
        ]
    count = sum(rows.shape[0] for _, rows in pairs)
    return pl.pallas_call(
        kernel,
        grid=(width // COMBINE,),
        in_specs=in_specs,
        out_specs=pl.BlockSpec((toks, COMBINE), lambda i: (0, i)),
        out_shape=jax.ShapeDtypeStruct((toks, width), F32),
        compiler_params=params(),
        cost_estimate=cost(4 * count * toks * width, 2 * count * width),
        name="combine",
    )(*[array for pair in pairs for array in pair])


def weigh_pack(bases, pers, pos, gm, weight, own, other, half):
    experts, toks = pos.shape
    width = own.shape[1]
    chunks = len(pers)
    tile = WEIGH
    counts = [experts * per // tile for per in pers]
    firsts = [sum(counts[:n]) for n in range(chunks)]

    def kernel(*refs):
        base_refs = refs[:chunks]
        blocks = refs[chunks : 3 * chunks]
        tw_ref, own_ref, other_ref = refs[3 * chunks : 3 * chunks + 3]
        outs = refs[3 * chunks + 3 : -2]
        tangent_ref, split_ref = refs[-2:]
        i = pl.program_id(0)

        @pl.when(i == 0)
        def _():
            cols = pl.ds(pl.multiple_of(base_refs[0][1] * half, half), half)
            tangent_ref[...] = (own_ref[:, cols] + other_ref[:, cols]).astype(BF)
            scale = jnp.broadcast_to(tw_ref[...], (toks, toks)).T[:, :1]
            scaled = scale * (own_ref[...] + other_ref[...])
            high = scaled.astype(BF)
            split_ref[:toks, :] = high
            split_ref[toks:, :] = (scaled - high.astype(F32)).astype(BF)

        for n in range(chunks):

            @pl.when((i >= firsts[n]) & (i < firsts[n] + counts[n]))
            def _(n=n):
                match = slot_match(blocks[2 * n][...], base_refs[n][0], pers[n])
                hot = jnp.where(match, 1.0, 0.0).astype(BF)
                gates = spread(blocks[2 * n + 1][...], pers[n])
                gate = jnp.sum(jnp.where(match, gates, 0.0), axis=1, keepdims=True)
                row = mm(jnp.concatenate([hot, hot], axis=1), split_ref[...])
                outs[n][...] = (gate * row).astype(BF)

    def at(n):
        return lambda i: (jnp.clip(i - firsts[n], 0, counts[n] - 1), 0)

    pos_specs = []
    for n, per in enumerate(pers):
        pos_specs += [pl.BlockSpec((tile // per, toks), at(n))] * 2
    return pl.pallas_call(
        kernel,
        grid=(sum(counts),),
        in_specs=[smem() for _ in bases]
        + pos_specs
        + [fixed((1, toks)), fixed((toks, width)), fixed((toks, width))],
        out_specs=[pl.BlockSpec((tile, width), at(n)) for n in range(chunks)]
        + [pl.BlockSpec((toks, half), lambda i: (0, 0))],
        out_shape=[jax.ShapeDtypeStruct((experts * per, width), BF) for per in pers]
        + [jax.ShapeDtypeStruct((toks, half), BF)],
        scratch_shapes=[pltpu.VMEM((2 * toks, width), BF)],
        compiler_params=params(),
        cost_estimate=cost(4 * experts * sum(pers) * toks * width, 2 * experts * sum(pers) * width),
        name="weigh_pack",
    )(*bases, *[array for _ in pers for array in (pos, gm)], weight, own, other)


def gradients(q, aux, down):
    count, width = q.shape
    hidden = down.shape[0]
    tile = min(TILE, count)

    def kernel(q_ref, silu_ref, us_ref, down_ref, g_ref):
        back = mm_t(q_ref[...], down_ref[...])
        g_ref[:, :hidden] = (back * us_ref[...]).astype(BF)
        g_ref[:, hidden:] = (back * silu_ref[...]).astype(BF)

    return pl.pallas_call(
        kernel,
        grid=(count // tile,),
        in_specs=[
            pl.BlockSpec((tile, width), lambda i: (i, 0)),
            pl.BlockSpec((tile, hidden), lambda i: (i, 1)),
            pl.BlockSpec((tile, hidden), lambda i: (i, 2)),
            fixed((hidden, width)),
        ],
        out_specs=pl.BlockSpec((tile, 2 * hidden), lambda i: (i, 0)),
        out_shape=jax.ShapeDtypeStruct((count, 2 * hidden), BF),
        compiler_params=params(),
        cost_estimate=cost(2 * count * width * hidden, 2 * count * width),
        name="gradients",
    )(q, aux, aux, down)


def phased_sums(own, other, down, factor):
    count, width = own[0].shape
    hidden = down.shape[0]
    tile = min(ROWS, count)
    piece = PIECE
    tiles = count // tile
    head = 2 * tiles

    def kernel(*refs):
        sides = (refs[:5], refs[5:10])
        down_ref = refs[10]
        outs = refs[11:14]
        g_ref, turned_ref, q_ref = refs[14:]
        i = pl.program_id(0)

        for side, (tile_ref, _, ad_ref, silu_ref, us_ref) in enumerate(sides):
            for n in range(tiles):

                @pl.when(i == side * tiles + n)
                def _(side=side, n=n, tile_ref=tile_ref, ad_ref=ad_ref, silu_ref=silu_ref, us_ref=us_ref):
                    rows = slice(side * count + n * tile, side * count + (n + 1) * tile)
                    q = tile_ref[...]
                    back = mm_t(q, down_ref[...])
                    g_ref[rows, :hidden] = (back * us_ref[...]).astype(BF)
                    g_ref[rows, hidden:] = (back * silu_ref[...]).astype(BF)
                    turned_ref[:, rows] = ad_ref[...].T
                    q_ref[rows, :] = q

        @pl.when(i >= head)
        def _():
            cols = pl.ds(pl.multiple_of(jnp.maximum(i - head, 0) * piece, piece), piece)
            gate_up = mm_rows(sides[0][1][...], g_ref[:count, :])
            gate_up += mm_rows(sides[1][1][...], g_ref[count:, :])
            outs[0][0] = (factor * gate_up[:, :hidden]).astype(BF)
            outs[1][0] = (factor * gate_up[:, hidden:]).astype(BF)
            outs[2][0] = (factor * mm(turned_ref[...], q_ref[:, cols])).astype(BF)

    def later(i):
        return jnp.maximum(i - head, 0)

    def specs(first):
        def at(i):
            return jnp.clip(i - first, 0, tiles - 1)

        return [
            pl.BlockSpec((tile, width), lambda i: (at(i), 0)),
            pl.BlockSpec((count, piece), lambda i: (0, later(i))),
            pl.BlockSpec((tile, hidden), lambda i: (at(i), 0)),
            pl.BlockSpec((tile, hidden), lambda i: (at(i), 1)),
            pl.BlockSpec((tile, hidden), lambda i: (at(i), 2)),
        ]

    shapes = [(1, width, hidden), (1, width, hidden), (1, hidden, width)]
    return pl.pallas_call(
        kernel,
        grid=(head + width // piece,),
        in_specs=specs(0) + specs(tiles) + [fixed((hidden, width))],
        out_specs=[
            pl.BlockSpec((1, piece, hidden), lambda i: (0, later(i), 0)),
            pl.BlockSpec((1, piece, hidden), lambda i: (0, later(i), 0)),
            pl.BlockSpec((1, hidden, piece), lambda i: (0, 0, later(i))),
        ],
        out_shape=[jax.ShapeDtypeStruct(shape, BF) for shape in shapes],
        scratch_shapes=[
            pltpu.VMEM((2 * count, 2 * hidden), BF),
            pltpu.VMEM((hidden, 2 * count), BF),
            pltpu.VMEM((2 * count, width), BF),
        ],
        compiler_params=params(),
        cost_estimate=cost(16 * count * width * hidden, 8 * count * width),
        name="phased_sums",
    )(*own, own[2], own[2], *other, other[2], other[2], down)


def last_sums(own, other, down, start, factor):
    count, width = own[0].shape
    hidden = down.shape[0]
    piece = LAST_PIECE

    def kernel(*refs):
        q_ref, x_ref, g_ref, act_ref, q2_ref, x2_ref, act2_ref, silu_ref, us_ref, down_ref = refs[:10]
        begins, outs = refs[10:13], refs[13:16]
        g2_ref, turned_ref = refs[16:]
        i = pl.program_id(0)

        @pl.when(i == 0)
        def _():
            back = mm_t(q2_ref[...], down_ref[...])
            g2_ref[:, :hidden] = (back * us_ref[...]).astype(BF)
            g2_ref[:, hidden:] = (back * silu_ref[...]).astype(BF)
            turned_ref[:, :count] = act_ref[...].T
            turned_ref[:, count:] = act2_ref[...].T

        cols = pl.ds(pl.multiple_of(i * piece, piece), piece)
        gate_up = mm_rows(x_ref[...], g_ref[...]) + mm_rows(x2_ref[...], g2_ref[...])
        below = mm(turned_ref[:, :count], q_ref[...]) + mm(turned_ref[:, count:], q2_ref[:, cols])
        terms = (gate_up[:, :hidden], gate_up[:, hidden:], below)
        for out, term, begin in zip(outs, terms, begins):
            out[0] = factor * term + begin[0].astype(F32)

    column = pl.BlockSpec((count, piece), lambda i: (0, i))

    def third(n):
        once = pl.Buffered(buffer_count=1)
        return pl.BlockSpec((count, hidden), lambda i: (0, n), pipeline_mode=once)

    results = [
        pl.BlockSpec((1, piece, hidden), lambda i: (0, i, 0)),
        pl.BlockSpec((1, piece, hidden), lambda i: (0, i, 0)),
        pl.BlockSpec((1, hidden, piece), lambda i: (0, 0, i)),
    ]
    shapes = [(1, width, hidden), (1, width, hidden), (1, hidden, width)]
    return pl.pallas_call(
        kernel,
        grid=(width // piece,),
        in_specs=[column, column, fixed((count, 2 * hidden)), third(0)]
        + [fixed((count, width)), column, third(0)]
        + [third(1), third(2), fixed((hidden, width))]
        + results,
        out_specs=results,
        out_shape=[jax.ShapeDtypeStruct(shape, F32) for shape in shapes],
        scratch_shapes=[
            pltpu.VMEM((count, 2 * hidden), BF),
            pltpu.VMEM((hidden, 2 * count), BF),
        ],
        compiler_params=params(),
        cost_estimate=cost(14 * count * width * hidden, 8 * count * width),
        name="last_sums",
    )(*own, *other, other[2], other[2], down, *start)


def exchange(rows):
    return lax.all_to_all(rows, GROUP, split_axis=0, concat_axis=0, tiled=True)


def body(tokens, expert_ids, gates, token_weight, w_gate, w_up, w_down, v_gate, v_up, v_down):
    toks, width = tokens.shape
    picks = expert_ids.shape[1]
    experts = lax.axis_size("dp") * lax.axis_size("expert")
    cores = lax.axis_size("tensor")
    hidden = w_gate.shape[2]
    per_core = min(3 * toks * picks // experts, toks) // cores
    core = lax.axis_index("tensor")
    factor = 1.0 / (toks * picks) ** 0.5

    def swap(rows):
        return lax.ppermute(rows, "tensor", [(0, 1), (1, 0)])

    chunks = []
    start = 0
    for per in SLOTS:
        size = per * per_core // sum(SLOTS)
        chunks.append((jnp.stack([core * per_core + start, core]).astype(jnp.int32), size))
        start += size

    base, per = chunks[0]
    packed, pos, gm = route_pack(base, expert_ids.T, gates.T, tokens, experts, per)
    arrived = exchange(packed)
    later = [pack(base, pos, tokens, per) for base, per in chunks[1:]]
    mats = jnp.concatenate([w_gate[0], w_up[0], v_gate[0], v_up[0]], axis=1)
    downs = jnp.concatenate([v_down[0], w_down[0]], axis=0)
    matrices = [gate_matrix(base, pos, gm, per) for base, per in chunks]
    arrived, later, mats, downs, matrices = lax.optimization_barrier(
        (arrived, later, mats, downs, matrices)
    )
    weight = token_weight[None, :]
    x_large = exchange(later[0])
    mats_other, downs_other = swap(mats), swap(downs)

    x_small = arrived
    part, aux_small, sent = forward(x_small, mats, mats_other, downs, downs_other)
    theirs_small = swap(x_small), swap(sent)
    x_large, part, theirs_small = lax.optimization_barrier((x_large, part, theirs_small))
    returned = exchange(part)
    x_their = swap(x_large)
    part, aux_large, sent = forward(x_large, mats, mats_other, downs, downs_other)
    returned, part, x_their = lax.optimization_barrier((returned, part, x_their))
    last = exchange(part)
    last, returned = lax.optimization_barrier((last, returned))
    own = combine(list(zip(matrices, (returned, last))))
    other = swap(own)

    order = (1, 0)
    bases, pers = zip(*[chunks[n] for n in order])
    send_large, send_small, tangent = weigh_pack(
        bases, pers, pos, gm, weight, own, other, width // cores
    )
    q_large = exchange(send_large)
    q_large, send_small, sent = lax.optimization_barrier((q_large, send_small, sent))
    q_small = exchange(send_small)
    down = w_down[0]
    sums = phased_sums(
        (q_large, x_large, aux_large), (swap(q_large), x_their, swap(sent)), down, factor
    )
    q_small, sums = lax.optimization_barrier((q_small, sums))
    q_other = swap(q_small)
    own_side = (q_small, x_small, gradients(q_small, aux_small, down), aux_small)
    gv_gate, gv_up, gv_down = last_sums(own_side, (q_other, *theirs_small), down, sums, factor)
    return gv_gate, gv_up, gv_down, tangent


def solution(mesh):
    rows = P(GROUP, None)
    cols = P(GROUP, None, "tensor")
    down = P(GROUP, "tensor", None)
    in_specs = (rows, rows, rows, P(GROUP), cols, cols, down, cols, cols, down)
    out_specs = (cols, cols, down, P(GROUP, "tensor"))
    return jax.shard_map(body, mesh=mesh, in_specs=in_specs, out_specs=out_specs, check_vma=False)
```

```python
import jax
import jax.numpy as jnp
from jax import lax
from jax.experimental import pallas as pl
from jax.experimental.pallas import tpu as pltpu
from jax.sharding import PartitionSpec as P

BF = jnp.bfloat16
F32 = jnp.float32
GROUP = ("dp", "expert")
VMEM_LIMIT = 63 * 1024 * 1024
TILE = 512
PIECE = 1024
LAST_PIECE = 512
ROWS = 512
SLOTS = (1, 2)
COMBINE = 1024
WEIGH = 512


def params():
    return pltpu.CompilerParams(
        dimension_semantics=("arbitrary",), vmem_limit_bytes=VMEM_LIMIT
    )


def cost(flops, nbytes):
    return pl.CostEstimate(flops=flops // 16, bytes_accessed=nbytes // 16, transcendentals=0)


def fixed(shape):
    return pl.BlockSpec(
        shape, lambda i: (0,) * len(shape), pipeline_mode=pl.Buffered(buffer_count=1)
    )


def smem():
    return pl.BlockSpec(memory_space=pltpu.SMEM)


def mm(left, right):
    return jnp.dot(left, right, preferred_element_type=F32)


def mm_t(left, right):
    return lax.dot_general(left, right, (((1,), (1,)), ((), ())), preferred_element_type=F32)


def mm_rows(left, right):
    return lax.dot_general(left, right, (((0,), (0,)), ((), ())), preferred_element_type=F32)


def spread(rows, per):
    count, toks = rows.shape
    return jnp.broadcast_to(rows[:, None, :], (count, per, toks)).reshape(count * per, toks)


def slot_match(pos, base, per):
    count, toks = pos.shape
    slot = lax.broadcasted_iota(jnp.int32, (count, per, toks), 1).reshape(count * per, toks)
    return spread(pos, per) == (slot + base).astype(F32)


def route_pack(base, ids_t, gates_t, tokens, experts, per):
    picks, toks = ids_t.shape
    width = tokens.shape[1]
    step = TILE // per
    steps = experts // step

    def kernel(base_ref, ids_ref, gates_ref, tok_ref, x_ref, pos_ref, gm_ref):
        i = pl.program_id(0)

        @pl.when(i == 0)
        def _():
            label = lax.broadcasted_iota(jnp.int32, (experts, toks), 0)
            hits = jnp.zeros((experts, toks), F32)
            gm = jnp.zeros((experts, toks), F32)
            for k in range(picks):
                match = ids_ref[k : k + 1, :] == label
                hits = jnp.where(match, 1.0, hits)
                gm = jnp.where(match, gates_ref[k : k + 1, :], gm)
            row = lax.broadcasted_iota(jnp.int32, (toks, toks), 0)
            col = lax.broadcasted_iota(jnp.int32, (toks, toks), 1)
            before = jnp.where(row < col, 1.0, 0.0).astype(BF)
            pos = mm(hits.astype(BF), before)
            pos_ref[...] = jnp.where(hits > 0.5, pos, -1.0)
            gm_ref[...] = gm

        pos = pos_ref[pl.ds(pl.multiple_of(i * step, step), step), :]
        hot = jnp.where(slot_match(pos, base_ref[0], per), 1.0, 0.0).astype(BF)
        x_ref[...] = mm(hot, tok_ref[...]).astype(BF)

    return pl.pallas_call(
        kernel,
        grid=(steps,),
        in_specs=[smem(), fixed((picks, toks)), fixed((picks, toks)), fixed((toks, width))],
        out_specs=[
            pl.BlockSpec((TILE, width), lambda i: (i, 0)),
            pl.BlockSpec((experts, toks), lambda i: (0, 0)),
            pl.BlockSpec((experts, toks), lambda i: (0, 0)),
        ],
        out_shape=[
            jax.ShapeDtypeStruct((experts * per, width), BF),
            jax.ShapeDtypeStruct((experts, toks), F32),
            jax.ShapeDtypeStruct((experts, toks), F32),
        ],
        compiler_params=params(),
        cost_estimate=cost(2 * experts * per * toks * width, 2 * experts * per * width),
        name="route_pack",
    )(base, ids_t, gates_t, tokens)


def pack(base, pos, tokens, per):
    experts, toks = pos.shape
    width = tokens.shape[1]
    step = TILE // per

    def kernel(base_ref, pos_ref, tok_ref, x_ref):
        hot = jnp.where(slot_match(pos_ref[...], base_ref[0], per), 1.0, 0.0).astype(BF)
        x_ref[...] = mm(hot, tok_ref[...]).astype(BF)

    return pl.pallas_call(
        kernel,
        grid=(experts // step,),
        in_specs=[smem(), pl.BlockSpec((step, toks), lambda i: (i, 0)), fixed((toks, width))],
        out_specs=pl.BlockSpec((TILE, width), lambda i: (i, 0)),
        out_shape=jax.ShapeDtypeStruct((experts * per, width), BF),
        compiler_params=params(),
        cost_estimate=cost(2 * experts * per * toks * width, 2 * experts * per * width),
        name="pack",
    )(base, pos, tokens)


def forward(rows, mats_own, mats_other, down_own, down_other):
    count, width = rows.shape
    hidden = mats_own.shape[1] // 4

    def kernel(x_ref, *refs):
        sources = refs[:4]
        part_ref, own_ref, other_ref = refs[4:7]
        held, sems = refs[7:11], refs[11]
        first = pl.program_id(0) == 0
        copies = [
            pltpu.make_async_copy(source, target, sems.at[n])
            for n, (source, target) in enumerate(zip(sources, held))
        ]

        @pl.when(first)
        def _():
            for copy in copies:
                copy.start()

        def ready(n):
            @pl.when(first)
            def _():
                copies[n].wait()

        def side(n, aux_ref):
            ready(n)
            pre = mm(x_ref[...], held[n][...])
            gate = pre[:, :hidden]
            up = pre[:, hidden : 2 * hidden]
            d_gate = pre[:, 2 * hidden : 3 * hidden]
            d_up = pre[:, 3 * hidden :]
            sigma = jax.nn.sigmoid(gate)
            silu = gate * sigma
            us = sigma * (1.0 + gate * (1.0 - sigma)) * up
            act = (silu * up).astype(BF)
            aux_ref[:, :hidden] = act
            aux_ref[:, hidden : 2 * hidden] = silu.astype(BF)
            aux_ref[:, 2 * hidden :] = us.astype(BF)
            d_act = (us * d_gate + silu * d_up).astype(BF)
            return jnp.concatenate([act, d_act], axis=1)

        left = side(0, own_ref)
        right = side(1, other_ref)
        ready(2)
        ready(3)
        part_ref[...] = (mm(left, held[2][...]) + mm(right, held[3][...])).astype(BF)

    weights = [mats_own, mats_other, down_own, down_other]
    return pl.pallas_call(
        kernel,
        grid=(count // TILE,),
        in_specs=[pl.BlockSpec((TILE, width), lambda i: (i, 0))]
        + [pl.BlockSpec(memory_space=pl.ANY) for _ in weights],
        out_specs=[
            pl.BlockSpec((TILE, width), lambda i: (i, 0)),
            pl.BlockSpec((TILE, 3 * hidden), lambda i: (i, 0)),
            pl.BlockSpec((TILE, 3 * hidden), lambda i: (i, 0)),
        ],
        out_shape=[
            jax.ShapeDtypeStruct((count, width), BF),
            jax.ShapeDtypeStruct((count, 3 * hidden), BF),
            jax.ShapeDtypeStruct((count, 3 * hidden), BF),
        ],
        scratch_shapes=[pltpu.VMEM(w.shape, BF) for w in weights]
        + [pltpu.SemaphoreType.DMA((len(weights),))],
        compiler_params=params(),
        cost_estimate=cost(24 * count * width * hidden, 8 * count * width),
        name="forward",
    )(rows, *weights)


def gate_matrix(base, pos, gm, per):
    experts, toks = pos.shape
    step = TILE // per

    def kernel(base_ref, pos_ref, gm_ref, out_ref):
        match = slot_match(pos_ref[...], base_ref[0], per)
        weight = jnp.where(match, spread(gm_ref[...], per), 0.0).T
        high = weight.astype(BF)
        out_ref[:toks, :] = high
        out_ref[toks:, :] = (weight - high.astype(F32)).astype(BF)

    return pl.pallas_call(
        kernel,
        grid=(experts // step,),
        in_specs=[
            smem(),
            pl.BlockSpec((step, toks), lambda i: (i, 0)),
            pl.BlockSpec((step, toks), lambda i: (i, 0)),
        ],
        out_specs=pl.BlockSpec((2 * toks, TILE), lambda i: (0, i)),
        out_shape=jax.ShapeDtypeStruct((2 * toks, experts * per), BF),
        compiler_params=params(),
        cost_estimate=cost(4 * experts * per * toks, 4 * experts * per * toks),
        name="gate_matrix",
    )(base, pos, gm)


def combine(pairs):
    width = pairs[0][1].shape[1]
    toks = pairs[0][0].shape[0] // 2

    def kernel(*refs):
        both = None
        for n in range(0, len(refs) - 1, 2):
            term = mm(refs[n][...], refs[n + 1][...])
            both = term if both is None else both + term
        refs[-1][...] = both[:toks] + both[toks:]

    in_specs = []
    for matrix, rows in pairs:
        in_specs += [
            fixed(matrix.shape),
            pl.BlockSpec((rows.shape[0], COMBINE), lambda i: (0, i)),
        ]
    count = sum(rows.shape[0] for _, rows in pairs)
    return pl.pallas_call(
        kernel,
        grid=(width // COMBINE,),
        in_specs=in_specs,
        out_specs=pl.BlockSpec((toks, COMBINE), lambda i: (0, i)),
        out_shape=jax.ShapeDtypeStruct((toks, width), F32),
        compiler_params=params(),
        cost_estimate=cost(4 * count * toks * width, 2 * count * width),
        name="combine",
    )(*[array for pair in pairs for array in pair])


def weigh_pack(bases, pers, pos, gm, weight, own, other, half):
    experts, toks = pos.shape
    width = own.shape[1]
    chunks = len(pers)
    tile = WEIGH
    counts = [experts * per // tile for per in pers]
    firsts = [sum(counts[:n]) for n in range(chunks)]

    def kernel(*refs):
        base_refs = refs[:chunks]
        blocks = refs[chunks : 3 * chunks]
        tw_ref, own_ref, other_ref = refs[3 * chunks : 3 * chunks + 3]
        outs = refs[3 * chunks + 3 : -2]
        tangent_ref, split_ref = refs[-2:]
        i = pl.program_id(0)

        @pl.when(i == 0)
        def _():
            cols = pl.ds(pl.multiple_of(base_refs[0][1] * half, half), half)
            tangent_ref[...] = (own_ref[:, cols] + other_ref[:, cols]).astype(BF)
            scale = jnp.broadcast_to(tw_ref[...], (toks, toks)).T[:, :1]
            scaled = scale * (own_ref[...] + other_ref[...])
            high = scaled.astype(BF)
            split_ref[:toks, :] = high
            split_ref[toks:, :] = (scaled - high.astype(F32)).astype(BF)

        for n in range(chunks):

            @pl.when((i >= firsts[n]) & (i < firsts[n] + counts[n]))
            def _(n=n):
                match = slot_match(blocks[2 * n][...], base_refs[n][0], pers[n])
                hot = jnp.where(match, 1.0, 0.0).astype(BF)
                gates = spread(blocks[2 * n + 1][...], pers[n])
                gate = jnp.sum(jnp.where(match, gates, 0.0), axis=1, keepdims=True)
                row = mm(jnp.concatenate([hot, hot], axis=1), split_ref[...])
                outs[n][...] = (gate * row).astype(BF)

    def at(n):
        return lambda i: (jnp.clip(i - firsts[n], 0, counts[n] - 1), 0)

    pos_specs = []
    for n, per in enumerate(pers):
        pos_specs += [pl.BlockSpec((tile // per, toks), at(n))] * 2
    return pl.pallas_call(
        kernel,
        grid=(sum(counts),),
        in_specs=[smem() for _ in bases]
        + pos_specs
        + [fixed((1, toks)), fixed((toks, width)), fixed((toks, width))],
        out_specs=[pl.BlockSpec((tile, width), at(n)) for n in range(chunks)]
        + [pl.BlockSpec((toks, half), lambda i: (0, 0))],
        out_shape=[jax.ShapeDtypeStruct((experts * per, width), BF) for per in pers]
        + [jax.ShapeDtypeStruct((toks, half), BF)],
        scratch_shapes=[pltpu.VMEM((2 * toks, width), BF)],
        compiler_params=params(),
        cost_estimate=cost(4 * experts * sum(pers) * toks * width, 2 * experts * sum(pers) * width),
        name="weigh_pack",
    )(*bases, *[array for _ in pers for array in (pos, gm)], weight, own, other)


def gradients(q, aux, down):
    count, width = q.shape
    hidden = down.shape[0]
    tile = min(TILE, count)

    def kernel(q_ref, silu_ref, us_ref, down_ref, g_ref):
        back = mm_t(q_ref[...], down_ref[...])
        g_ref[:, :hidden] = (back * us_ref[...]).astype(BF)
        g_ref[:, hidden:] = (back * silu_ref[...]).astype(BF)

    return pl.pallas_call(
        kernel,
        grid=(count // tile,),
        in_specs=[
            pl.BlockSpec((tile, width), lambda i: (i, 0)),
            pl.BlockSpec((tile, hidden), lambda i: (i, 1)),
            pl.BlockSpec((tile, hidden), lambda i: (i, 2)),
            fixed((hidden, width)),
        ],
        out_specs=pl.BlockSpec((tile, 2 * hidden), lambda i: (i, 0)),
        out_shape=jax.ShapeDtypeStruct((count, 2 * hidden), BF),
        compiler_params=params(),
        cost_estimate=cost(2 * count * width * hidden, 2 * count * width),
        name="gradients",
    )(q, aux, aux, down)


def phased_sums(own, other, down, factor):
    count, width = own[0].shape
    hidden = down.shape[0]
    tile = min(ROWS, count)
    piece = PIECE
    tiles = count // tile
    head = 2 * tiles

    def kernel(*refs):
        sides = (refs[:5], refs[5:10])
        down_ref = refs[10]
        outs = refs[11:14]
        g_ref, turned_ref, q_ref = refs[14:]
        i = pl.program_id(0)

        for side, (tile_ref, _, ad_ref, silu_ref, us_ref) in enumerate(sides):
            for n in range(tiles):

                @pl.when(i == side * tiles + n)
                def _(side=side, n=n, tile_ref=tile_ref, ad_ref=ad_ref, silu_ref=silu_ref, us_ref=us_ref):
                    rows = slice(side * count + n * tile, side * count + (n + 1) * tile)
                    q = tile_ref[...]
                    back = mm_t(q, down_ref[...])
                    g_ref[rows, :hidden] = (back * us_ref[...]).astype(BF)
                    g_ref[rows, hidden:] = (back * silu_ref[...]).astype(BF)
                    turned_ref[:, rows] = ad_ref[...].T
                    q_ref[rows, :] = q

        @pl.when(i >= head)
        def _():
            cols = pl.ds(pl.multiple_of(jnp.maximum(i - head, 0) * piece, piece), piece)
            gate_up = mm_rows(sides[0][1][...], g_ref[:count, :])
            gate_up += mm_rows(sides[1][1][...], g_ref[count:, :])
            outs[0][0] = (factor * gate_up[:, :hidden]).astype(BF)
            outs[1][0] = (factor * gate_up[:, hidden:]).astype(BF)
            outs[2][0] = (factor * mm(turned_ref[...], q_ref[:, cols])).astype(BF)

    def later(i):
        return jnp.maximum(i - head, 0)

    def specs(first):
        def at(i):
            return jnp.clip(i - first, 0, tiles - 1)

        return [
            pl.BlockSpec((tile, width), lambda i: (at(i), 0)),
            pl.BlockSpec((count, piece), lambda i: (0, later(i))),
            pl.BlockSpec((tile, hidden), lambda i: (at(i), 0)),
            pl.BlockSpec((tile, hidden), lambda i: (at(i), 1)),
            pl.BlockSpec((tile, hidden), lambda i: (at(i), 2)),
        ]

    shapes = [(1, width, hidden), (1, width, hidden), (1, hidden, width)]
    return pl.pallas_call(
        kernel,
        grid=(head + width // piece,),
        in_specs=specs(0) + specs(tiles) + [fixed((hidden, width))],
        out_specs=[
            pl.BlockSpec((1, piece, hidden), lambda i: (0, later(i), 0)),
            pl.BlockSpec((1, piece, hidden), lambda i: (0, later(i), 0)),
            pl.BlockSpec((1, hidden, piece), lambda i: (0, 0, later(i))),
        ],
        out_shape=[jax.ShapeDtypeStruct(shape, BF) for shape in shapes],
        scratch_shapes=[
            pltpu.VMEM((2 * count, 2 * hidden), BF),
            pltpu.VMEM((hidden, 2 * count), BF),
            pltpu.VMEM((2 * count, width), BF),
        ],
        compiler_params=params(),
        cost_estimate=cost(16 * count * width * hidden, 8 * count * width),
        name="phased_sums",
    )(*own, own[2], own[2], *other, other[2], other[2], down)


def last_sums(own, other, down, start, factor):
    count, width = own[0].shape
    hidden = down.shape[0]
    piece = LAST_PIECE

    def kernel(*refs):
        q_ref, x_ref, g_ref, act_ref, q2_ref, x2_ref, act2_ref, silu_ref, us_ref, down_ref = refs[:10]
        begins, outs = refs[10:13], refs[13:16]
        g2_ref, turned_ref = refs[16:]
        i = pl.program_id(0)

        @pl.when(i == 0)
        def _():
            back = mm_t(q2_ref[...], down_ref[...])
            g2_ref[:, :hidden] = (back * us_ref[...]).astype(BF)
            g2_ref[:, hidden:] = (back * silu_ref[...]).astype(BF)
            turned_ref[:, :count] = act_ref[...].T
            turned_ref[:, count:] = act2_ref[...].T

        cols = pl.ds(pl.multiple_of(i * piece, piece), piece)
        gate_up = mm_rows(x_ref[...], g_ref[...]) + mm_rows(x2_ref[...], g2_ref[...])
        below = mm(turned_ref[:, :count], q_ref[...]) + mm(turned_ref[:, count:], q2_ref[:, cols])
        terms = (gate_up[:, :hidden], gate_up[:, hidden:], below)
        for out, term, begin in zip(outs, terms, begins):
            out[0] = factor * term + begin[0].astype(F32)

    column = pl.BlockSpec((count, piece), lambda i: (0, i))

    def third(n):
        once = pl.Buffered(buffer_count=1)
        return pl.BlockSpec((count, hidden), lambda i: (0, n), pipeline_mode=once)

    results = [
        pl.BlockSpec((1, piece, hidden), lambda i: (0, i, 0)),
        pl.BlockSpec((1, piece, hidden), lambda i: (0, i, 0)),
        pl.BlockSpec((1, hidden, piece), lambda i: (0, 0, i)),
    ]
    shapes = [(1, width, hidden), (1, width, hidden), (1, hidden, width)]
    return pl.pallas_call(
        kernel,
        grid=(width // piece,),
        in_specs=[column, column, fixed((count, 2 * hidden)), third(0)]
        + [fixed((count, width)), column, third(0)]
        + [third(1), third(2), fixed((hidden, width))]
        + results,
        out_specs=results,
        out_shape=[jax.ShapeDtypeStruct(shape, F32) for shape in shapes],
        scratch_shapes=[
            pltpu.VMEM((count, 2 * hidden), BF),
            pltpu.VMEM((hidden, 2 * count), BF),
        ],
        compiler_params=params(),
        cost_estimate=cost(14 * count * width * hidden, 8 * count * width),
        name="last_sums",
    )(*own, *other, other[2], other[2], down, *start)


def exchange(rows):
    return lax.all_to_all(rows, GROUP, split_axis=0, concat_axis=0, tiled=True)


def body(tokens, expert_ids, gates, token_weight, w_gate, w_up, w_down, v_gate, v_up, v_down):
    toks, width = tokens.shape
    picks = expert_ids.shape[1]
    experts = lax.axis_size("dp") * lax.axis_size("expert")
    cores = lax.axis_size("tensor")
    hidden = w_gate.shape[2]
    per_core = min(3 * toks * picks // experts, toks) // cores
    core = lax.axis_index("tensor")
    factor = 1.0 / (toks * picks) ** 0.5

    def swap(rows):
        return lax.ppermute(rows, "tensor", [(0, 1), (1, 0)])

    chunks = []
    start = 0
    for per in SLOTS:
        size = per * per_core // sum(SLOTS)
        chunks.append((jnp.stack([core * per_core + start, core]).astype(jnp.int32), size))
        start += size

    base, per = chunks[0]
    packed, pos, gm = route_pack(base, expert_ids.T, gates.T, tokens, experts, per)
    arrived = exchange(packed)
    later = [pack(base, pos, tokens, per) for base, per in chunks[1:]]
    mats = jnp.concatenate([w_gate[0], w_up[0], v_gate[0], v_up[0]], axis=1)
    downs = jnp.concatenate([v_down[0], w_down[0]], axis=0)
    matrices = [gate_matrix(base, pos, gm, per) for base, per in chunks]
    arrived, later, mats, downs, matrices = lax.optimization_barrier(
        (arrived, later, mats, downs, matrices)
    )
    weight = token_weight[None, :]
    x_large = exchange(later[0])
    mats_other, downs_other = swap(mats), swap(downs)

    x_small = arrived
    part, aux_small, sent = forward(x_small, mats, mats_other, downs, downs_other)
    theirs_small = swap(x_small), swap(sent)
    x_large, part, theirs_small = lax.optimization_barrier((x_large, part, theirs_small))
    returned = exchange(part)
    x_their = swap(x_large)
    part, aux_large, sent = forward(x_large, mats, mats_other, downs, downs_other)
    returned, part, x_their = lax.optimization_barrier((returned, part, x_their))
    last = exchange(part)
    last, returned = lax.optimization_barrier((last, returned))
    own = combine(list(zip(matrices, (returned, last))))
    other = swap(own)

    order = (1, 0)
    bases, pers = zip(*[chunks[n] for n in order])
    send_large, send_small, tangent = weigh_pack(
        bases, pers, pos, gm, weight, own, other, width // cores
    )
    q_large = exchange(send_large)
    q_large, send_small, sent = lax.optimization_barrier((q_large, send_small, sent))
    q_small = exchange(send_small)
    down = w_down[0]
    sums = phased_sums(
        (q_large, x_large, aux_large), (swap(q_large), x_their, swap(sent)), down, factor
    )
    q_small, sums = lax.optimization_barrier((q_small, sums))
    q_other = swap(q_small)
    own_side = (q_small, x_small, gradients(q_small, aux_small, down), aux_small)
    gv_gate, gv_up, gv_down = last_sums(own_side, (q_other, *theirs_small), down, sums, factor)
    return gv_gate, gv_up, gv_down, tangent


def solution(mesh):
    rows = P(GROUP, None)
    cols = P(GROUP, None, "tensor")
    down = P(GROUP, "tensor", None)
    in_specs = (rows, rows, rows, P(GROUP), cols, cols, down, cols, cols, down)
    out_specs = (cols, cols, down, P(GROUP, "tensor"))
    return jax.shard_map(body, mesh=mesh, in_specs=in_specs, out_specs=out_specs, check_vma=False)
```
